32 devices in a mesh: gx: 4 (over y, x), gy: 4 (over z), gz: 2 (over core).
Axes of the slice: x: 2, y: 2, z: 4, core: 2. Of those that a mesh axis runs over, the one named last changes fastest.
Arguments:
- solution_old: float32 [128, 32, 1024], P(('gx', 'gy', 'gz')), may hold values from -6 to 6
- right_side: float32 [128, 32, 1024], P(('gx', 'gy', 'gz')), may hold values from -6 to 6
- acoef: float32 [128, 32, 1024], P(('gx', 'gy', 'gz')), may hold values from 0.05 to 1
- bcoef: float32 [128, 32, 1024], P(('gx', 'gy', 'gz')), may hold values from 0.25 to 4
- corners: int32 [3, 128], replicated, may hold values from 0 to 224, as said below
Outputs:
- solution: float32 [128, 128, 256], P('gx', 'gy', 'gz')
- residual: float32 [128, 128, 256], P('gx', 'gy', 'gz')
The draws below stay inside these ranges and needn't reach their ends.
Inputs may be any that keep to these rules, and one draw needn't show every extreme that they name: `corners`: each corner is a multiple of 32 in every dimension and the boxes tile the level one to one. The new owner of a box, the device whose block of 32 x 32 x 128 cells holds its corner, has the same gx and gz indices as the device that holds its row. At most one box moves from one device to any other device, and at most min(3, 3) boxes leave or reach one device; in each group of devices with one gx and one gz index, one device swaps a box with each of that many others, and every other device of the group passes one box on along a cycle through them.
All inputs are finite; a program needn't handle non-finite values.
Results may differ from the reference program's by a relative error of at most 0.00002.
Values sent between devices are 32-bit elements; how exact they have to be, the bound alone decides.
A program may use at most 64 MiB of HBM per device.

```python
import math
import jax
import jax.numpy as jnp
from jax import lax

BOX = 32
BXB = 1
BYB = 1
BZB = 4
SWEEPS = 2
NB = 128
NX = 128
NY = 128
NZ = 256
N_GX = 4
N_GY = 4
N_GZ = 2


def draw_corners(key, part):
    group = N_GY
    groups_n = N_GX * N_GZ
    per_dev = BXB * BYB * BZB
    others_n = group - 1
    hot_n = min(per_dev - 1, others_n)
    key_hot, key_order, key_perm = jax.random.split(key, 3)
    hot_dev = jax.random.randint(key_hot, (groups_n,), 0, group).astype(jnp.int32)

    def ordered(one_key):
        return jax.random.permutation(one_key, others_n).astype(jnp.int32)

    def shuffled(one_key):
        return jax.random.permutation(one_key, per_dev).astype(jnp.int32)
    order = jax.vmap(ordered)(jax.random.split(key_order, groups_n))
    order_inv = jnp.argsort(order, axis=1).astype(jnp.int32)
    perms = jax.vmap(shuffled)(jax.random.split(key_perm, groups_n * group)).reshape(groups_n, group, per_dev)
    inverse = jnp.argsort(perms, axis=2).astype(jnp.int32)
    full_shape = (groups_n, group, per_dev)
    group_id = jnp.arange(groups_n, dtype=jnp.int32)[:, None, None]
    device = jnp.broadcast_to(jnp.arange(group, dtype=jnp.int32)[None, :, None], full_shape)
    position = jnp.broadcast_to(jnp.arange(per_dev, dtype=jnp.int32)[None, None, :], full_shape)
    group_full = jnp.broadcast_to(group_id, full_shape)
    hot_here = jnp.broadcast_to(hot_dev[:, None, None], full_shape)
    is_hot = device == hot_here
    rel = (device - hot_here - 1) % group
    cyc = order_inv[group_full, jnp.minimum(rel, others_n - 1)]
    rank = inverse
    src_dev = device
    src_slot = position
    in_set = jnp.logical_not(is_hot) & (cyc < hot_n)
    from_hot = in_set & (rank == 0)
    src_dev = jnp.where(from_hot, hot_here, src_dev)
    src_slot = jnp.where(from_hot, perms[group_full, hot_here, jnp.minimum(cyc, per_dev - 1)], src_slot)
    if others_n >= 2:
        pred_rel = order[group_full, (cyc - 1) % others_n]
        pred = (hot_here + 1 + pred_rel) % group
        by_cycle = jnp.logical_not(is_hot) & (rank == 1)
        src_dev = jnp.where(by_cycle, pred, src_dev)
        src_slot = jnp.where(by_cycle, perms[group_full, pred, 1], src_slot)
    to_hot = is_hot & (rank < hot_n)
    peer = (hot_here + 1 + order[group_full, jnp.minimum(rank, others_n - 1)]) % group
    src_dev = jnp.where(to_hot, peer, src_dev)
    src_slot = jnp.where(to_hot, perms[group_full, peer, 0], src_slot)
    index_x = group_full // N_GZ
    index_z = group_full % N_GZ
    old_index = ((index_x * N_GY + src_dev) * N_GZ + index_z) * per_dev + src_slot
    box_x = position // (BYB * BZB)
    box_y = position // BZB % BYB
    box_z = position % BZB
    corner_x = index_x * (BXB * BOX) + box_x * BOX
    corner_y = device * (BYB * BOX) + box_y * BOX
    corner_z = index_z * (BZB * BOX) + box_z * BOX
    stacked = jnp.stack([corner_x, corner_y, corner_z]).reshape(3, -1).astype(jnp.int32)
    total = groups_n * group * per_dev
    return jnp.zeros((3, total), jnp.int32).at[:, old_index.reshape(-1)].set(stacked)


def block_levels(stream_key, extent, shards, least, largest):
    def one(dim, blocks):
        draws = jax.random.uniform(jax.random.fold_in(jax.random.fold_in(stream_key, 6), dim), (blocks,), jnp.float32, least / len(shards), largest / len(shards))
        return jnp.repeat(jnp.exp(draws), extent[dim] // blocks).reshape((-1,) + (1,) * (len(extent) - dim - 1))

    loudness = one(*shards[0])
    for cut in shards[1:]:
        loudness = loudness * one(*cut)
    return loudness


def scatter_about(rng, shape, scale, most, pieces=(), held_as=jnp.bfloat16):
    factor_of = block_levels(rng, shape, pieces, -0.22, 0.18) if pieces else 1.0
    result = jax.random.normal(rng, shape, jnp.float32) * scale * factor_of
    return jnp.minimum(jnp.maximum(result, -most), most).astype(held_as)


def setup_inputs(seed: int = 0) -> dict:
    seeds = jax.random.split(jax.random.key(seed), 6)
    solution_old = scatter_about(seeds[0], (NB, BOX, BOX * BOX), 1.0, 6.0, ((0, 32),), jnp.float32)
    right_side = scatter_about(seeds[1], (NB, BOX, BOX * BOX), 1.0, 6.0, ((0, 32),), jnp.float32)
    acoef = jnp.clip(jnp.exp(math.log(1.0) - 2.9957323 * jax.random.uniform(seeds[2], (NB, BOX, BOX * BOX), jnp.float32) ** block_levels(seeds[2], (NB, BOX, BOX * BOX), ((0, 32),), -0.2, 0.2)), 0.05, 1.0)
    bcoef = jnp.clip(jnp.exp(math.log(4.0) - 2.7725887 * jax.random.uniform(seeds[3], (NB, BOX, BOX * BOX), jnp.float32) ** block_levels(seeds[3], (NB, BOX, BOX * BOX), ((0, 32),), -0.2, 0.2)), 0.25, 4.0)
    corners = draw_corners(jax.random.fold_in(seeds[5], 71), 0)
    return {"solution_old": solution_old, "right_side": right_side, "acoef": acoef, "bcoef": bcoef, "corners": corners}


def place_boxes(boxes, box_order):
    grouped = boxes[box_order].reshape(NX // BOX, NY // BOX, NZ // BOX, BOX, BOX, BOX)
    return grouped.transpose(0, 3, 1, 4, 2, 5).reshape(NX, NY, NZ)


def face_coefs(padded):
    face_x = 0.5 * (padded[1:, 1:-1, 1:-1] + padded[:-1, 1:-1, 1:-1])
    face_y = 0.5 * (padded[1:-1, 1:, 1:-1] + padded[1:-1, :-1, 1:-1])
    face_z = 0.5 * (padded[1:-1, 1:-1, 1:] + padded[1:-1, 1:-1, :-1])
    return face_x, face_y, face_z


def diag_of(absorb, face_set):
    face_x, face_y, face_z = face_set
    return absorb + (face_x[1:] + face_x[:-1]) + (face_y[:, 1:] + face_y[:, :-1]) + (face_z[:, :, 1:] + face_z[:, :, :-1])


def neighbors(padded, face_set):
    face_x, face_y, face_z = face_set
    summed = face_x[1:] * padded[2:, 1:-1, 1:-1] + face_x[:-1] * padded[:-2, 1:-1, 1:-1]
    summed = summed + face_y[:, 1:] * padded[1:-1, 2:, 1:-1] + face_y[:, :-1] * padded[1:-1, :-2, 1:-1]
    summed = summed + face_z[:, :, 1:] * padded[1:-1, 1:-1, 2:] + face_z[:, :, :-1] * padded[1:-1, 1:-1, :-2]
    return summed


def checker(grid_shape):
    return (lax.broadcasted_iota(jnp.int32, grid_shape, 0) + lax.broadcasted_iota(jnp.int32, grid_shape, 1) + lax.broadcasted_iota(jnp.int32, grid_shape, 2)) % 2


def reference(solution_old, right_side, acoef, bcoef, corners):
    box_cells = corners // BOX
    flat_index = (box_cells[0] * (NY // BOX) + box_cells[1]) * (NZ // BOX) + box_cells[2]
    box_order = jnp.zeros((NB,), jnp.int32).at[flat_index].set(jnp.arange(NB, dtype=jnp.int32))
    solution = place_boxes(solution_old, box_order)
    forcing = place_boxes(right_side, box_order)
    absorb = place_boxes(acoef, box_order)
    diffuse = place_boxes(bcoef, box_order)
    face_set = face_coefs(jnp.pad(diffuse, 1))
    diagonal = diag_of(absorb, face_set)
    parity = checker((NX, NY, NZ))
    for sweep_no in range(SWEEPS):
        for colour in (0, 1):
            updated = (forcing + neighbors(jnp.pad(solution, 1), face_set)) / diagonal
            solution = jnp.where(parity == colour, updated, solution)
    residual = forcing - (diagonal * solution - neighbors(jnp.pad(solution, 1), face_set))
    return solution, residual
```

```python
import functools

import jax
import jax.numpy as jnp
from jax import lax
from jax.experimental import pallas as pl
from jax.experimental.pallas import tpu as pltpu
from jax.sharding import PartitionSpec as P

SWEEPS = 2
E = 32
L = 128
PER = 4
MESH = pl.DeviceIdType.MESH
SIDES = (("gx", -1), ("gx", 1), ("gy", -1), ("gy", 1), ("gz", -1), ("gz", 1))


def kernel(
    width,
    corners,
    sol_in,
    rhs_in,
    abs_in,
    dif_in,
    sol_out,
    res_out,
    own_b,
    own_u,
    own_a,
    own_f,
    st_b,
    st_u,
    st_a,
    st_f,
    rv_b,
    rv_u,
    rv_a,
    rv_f,
    b,
    u,
    f,
    dia,
    inv,
    res,
    cxl,
    cxh,
    cy,
    czl,
    czh,
    hs,
    hr,
    in_sem,
    ms_sem,
    mr_sem,
    hs_sem,
    hr_sem,
):
    me = {axis: lax.axis_index(axis) for axis in ("gx", "gy", "gz")}
    n_y = width["gy"]
    my_y = me["gy"]

    loads = [
        pltpu.make_async_copy(src, dst, in_sem.at[i])
        for i, (src, dst) in enumerate(
            ((dif_in, own_b), (sol_in, own_u), (abs_in, own_a), (rhs_in, own_f))
        )
    ]
    for load in loads:
        load.start()

    def exists(side):
        axis, step = SIDES[side]
        return me[axis] > 0 if step < 0 else me[axis] < width[axis] - 1

    hr[...] = jnp.zeros_like(hr)

    barrier = pltpu.get_barrier_semaphore()
    partners = n_y - 1
    for k in range(1, n_y):
        pl.semaphore_signal(
            barrier, inc=1, device_id={"gy": lax.rem(my_y + k, n_y)}, device_id_type=MESH
        )
    for side in (0, 1, 4, 5):
        axis, step = SIDES[side]

        @pl.when(exists(side))
        def _():
            pl.semaphore_signal(
                barrier, inc=1, device_id={axis: me[axis] + step}, device_id_type=MESH
            )

        partners = partners + exists(side).astype(jnp.int32)

    def owner_inner(device, slot):
        row = ((me["gx"] * n_y + device) * width["gz"] + me["gz"]) * PER + slot
        return corners[1, row] // E, lax.rem(corners[2, row], PER * E) // E

    mine = [owner_inner(my_y, s) for s in range(PER)]
    send_slot = []
    for k in range(1, n_y):
        target = lax.rem(my_y + k, n_y)
        slot = jnp.int32(0)
        for s in range(PER):
            slot = jnp.where(mine[s][0] == target, s, slot)
        send_slot.append(slot)
    own_slot = [jnp.int32(0)] * PER
    is_own = [jnp.int32(0)] * PER
    got_slot = [jnp.int32(0)] * PER
    for q in range(PER):
        for s in range(PER):
            here = (mine[s][0] == my_y) & (mine[s][1] == q)
            own_slot[q] = jnp.where(here, s, own_slot[q])
            is_own[q] = jnp.where(here, 1, is_own[q])
    for k in range(1, n_y):
        device = lax.rem(my_y + n_y - k, n_y)
        for s in range(PER):
            owner, inner = owner_inner(device, s)
            for q in range(PER):
                got_slot[q] = jnp.where((owner == my_y) & (inner == q), k - 1, got_slot[q])

    row = lax.broadcasted_iota(jnp.int32, (E, L), 0)
    lane = lax.broadcasted_iota(jnp.int32, (E, L), 1)
    wide_row = lax.broadcasted_iota(jnp.int32, (E // 2, E * E), 0)
    wide_lane = lax.broadcasted_iota(jnp.int32, (E // 2, E * E), 1)
    odd_half = (wide_row + wide_lane // E + wide_lane) % 2 == 1

    def migrate(i, k, st, rv):
        return pltpu.make_async_remote_copy(
            src_ref=st.at[k - 1],
            dst_ref=rv.at[k - 1],
            send_sem=ms_sem.at[i, k - 1],
            recv_sem=mr_sem.at[i, k - 1],
            device_id={"gy": lax.rem(my_y + k, n_y)},
            device_id_type=MESH,
        )

    fields = ((own_b, st_b, rv_b), (own_u, st_u, rv_u), (own_a, st_a, rv_a), (own_f, st_f, rv_f))
    for i, (own, st, rv) in enumerate(fields):
        loads[i].wait()
        for k in range(1, n_y):
            box = own[send_slot[k - 1]]
            if i == 1:
                box = jnp.where(odd_half, box[: E // 2], pltpu.roll(box[E // 2 :], 1, 0))
            st[k - 1] = box
        if i == 0:
            pl.semaphore_wait(barrier, partners)
        for k in range(1, n_y):
            migrate(i, k, st, rv).start()

    def arrived(i):
        _, st, rv = fields[i]
        for k in range(1, n_y):
            migrate(i, k, st, rv).wait_recv()

    group = lane // E
    own_mask = [jnp.full((E, L), is_own[q], jnp.int32) == 1 for q in range(PER)]

    def assembled(i, put):
        own, _, rv = fields[i]

        def columns(t, carry):
            at = pl.ds(pl.multiple_of(t * L, L), L)
            parts = []
            for q in range(PER):
                got = rv[got_slot[q], :, at]
                if i == 1:
                    got = jnp.concatenate([got, pltpu.roll(got, E // 2 - 1, 0)], axis=0)
                parts.append(jnp.where(own_mask[q], own[own_slot[q], :, at], got))
            for j in range(PER):
                plane = parts[j]
                for q in range(PER):
                    if q != j:
                        plane = jnp.where(
                            group == q, pltpu.roll(parts[q], (q - j) * E % L, 1), plane
                        )
                put(t * PER + j, plane)
            return carry

        lax.fori_loop(0, E * E // L, columns, 0)

    def at_plane(y):
        return pl.ds(pl.multiple_of(y * E, E), E)

    def z_face(y, v, low, high):
        low = jnp.where(lane == y, pltpu.roll(v, y, 1), low)
        high = jnp.where(lane == y, pltpu.roll(v, y + 1, 1), high)
        return low, high

    def pack_z(ref):
        def planes(t, faces):
            for j in range(4):
                y = t * 4 + j
                faces = z_face(y, ref[at_plane(y + 1), :], *faces)
            return faces

        zero = jnp.zeros((E, L), jnp.float32)
        return lax.fori_loop(0, E // 4, planes, (zero, zero))

    def face_copy(e, side):
        axis, step = SIDES[side]
        return pltpu.make_async_remote_copy(
            src_ref=hs.at[e, side],
            dst_ref=hr.at[e, side ^ 1],
            send_sem=hs_sem.at[e, side],
            recv_sem=hr_sem.at[e, side ^ 1],
            device_id={axis: me[axis] + step},
            device_id_type=MESH,
        )

    def send_faces(e, ref, z_faces):
        hs[e, 0] = ref[pl.ds(E, E, stride=E), :]
        hs[e, 1] = ref[pl.ds(2 * E - 1, E, stride=E), :]
        hs[e, 2] = ref[pl.ds(E, E), :]
        hs[e, 3] = ref[pl.ds(E * E, E), :]
        hs[e, 4] = z_faces[0]
        hs[e, 5] = z_faces[1]
        for side in range(6):

            @pl.when(exists(side))
            def _():
                face_copy(e, side).start()

    def take_faces(e, ref):
        for side in range(6):
            axis, step = SIDES[side]

            @pl.when(exists(side))
            def _():
                pltpu.make_async_remote_copy(
                    src_ref=hs.at[e, side],
                    dst_ref=hr.at[e, side],
                    send_sem=hs_sem.at[e, side],
                    recv_sem=hr_sem.at[e, side],
                    device_id={axis: me[axis] + step},
                    device_id_type=MESH,
                ).wait_recv()

        ref[pl.ds(0, E), :] = hr[e, 2]
        ref[pl.ds((E + 1) * E, E), :] = hr[e, 3]

    def around(e, ref, y):
        v = ref[at_plane(y + 1), :]
        x_low = jnp.where(row == 0, hr[e, 0, pl.ds(y, 1), :], pltpu.roll(v, 1, 0))
        x_high = jnp.where(row == E - 1, hr[e, 1, pl.ds(y, 1), :], pltpu.roll(v, E - 1, 0))
        y_low = ref[at_plane(y), :]
        y_high = ref[at_plane(y + 2), :]
        z_low = jnp.where(
            lane == 0, pltpu.roll(hr[e, 4], lax.rem(L - y, L), 1), pltpu.roll(v, 1, 1)
        )
        z_high = jnp.where(
            lane == L - 1, pltpu.roll(hr[e, 5], L - 1 - y, 1), pltpu.roll(v, L - 1, 1)
        )
        return v, x_low, x_high, y_low, y_high, z_low, z_high

    arrived(0)

    def put_b(y, plane):
        b[at_plane(y + 1), :] = plane

    assembled(0, put_b)
    send_faces(0, b, pack_z(b))

    arrived(1)

    def put_u(y, plane):
        u[at_plane(y + 1), :] = plane

    assembled(1, put_u)
    send_faces(1, u, pack_z(u))

    take_faces(0, b)

    def coefs(y, carry):
        v, x_low, x_high, y_low, y_high, z_low, z_high = around(0, b, y)
        at = at_plane(y)
        x_low = 0.5 * (x_low + v)
        x_high = 0.5 * (x_high + v)
        y_low = 0.5 * (y_low + v)
        y_high = 0.5 * (y_high + v)
        z_low = 0.5 * (z_low + v)
        z_high = 0.5 * (z_high + v)
        cxl[at, :] = x_low
        cxh[at, :] = x_high
        cy[at, :] = y_low
        cy[at_plane(y + 1), :] = y_high
        czl[at, :] = z_low
        czh[at, :] = z_high
        dia[at, :] = (x_high + x_low) + (y_high + y_low) + (z_high + z_low)
        return carry

    lax.fori_loop(0, E, coefs, 0)

    arrived(2)

    def put_a(y, plane):
        at = at_plane(y)
        total = plane + dia[at, :]
        dia[at, :] = total
        inv[at, :] = 1.0 / total

    assembled(2, put_a)
    arrived(3)

    def put_f(y, plane):
        f[at_plane(y), :] = plane

    assembled(3, put_f)

    def neighbours(e, y):
        v, x_low, x_high, y_low, y_high, z_low, z_high = around(e, u, y)
        at = at_plane(y)
        total = cxh[at, :] * x_high + cxl[at, :] * x_low
        total = total + (cy[at_plane(y + 1), :] * y_high + cy[at, :] * y_low)
        total = total + (czh[at, :] * z_high + czl[at, :] * z_low)
        return v, total

    e = 1
    for sweep in range(SWEEPS):
        for colour in (0, 1):
            take_faces(e, u)

            def planes(t, faces):
                for j in range(4):
                    y = t * 4 + j
                    at = at_plane(y)
                    v, total = neighbours(e, y)
                    new = (f[at, :] + total) * inv[at, :]
                    v = jnp.where((row + lane + j) % 2 == colour, new, v)
                    u[at_plane(y + 1), :] = v
                    faces = z_face(y, v, *faces)
                return faces

            zero = jnp.zeros((E, L), jnp.float32)
            faces = lax.fori_loop(0, E // 4, planes, (zero, zero))
            e += 1
            send_faces(e, u, faces)

    for x in range(E):
        sol_out[x] = u[pl.ds(E + x, E, stride=E), :]
    take_faces(e, u)

    def residual(y, carry):
        at = at_plane(y)
        v, total = neighbours(e, y)
        res[at, :] = f[at, :] - (dia[at, :] * v - total)
        return carry

    lax.fori_loop(0, E, residual, 0)
    for x in range(E):
        res_out[x] = res[pl.ds(x, E, stride=E), :]

    for i, (_, st, rv) in enumerate(fields):
        for k in range(1, n_y):
            migrate(i, k, st, rv).wait_send()
    for exchange in range(e + 1):
        for side in range(6):

            @pl.when(exists(side))
            def _():
                face_copy(exchange, side).wait_send()


def per_device(width, solution_old, right_side, acoef, bcoef, corners):
    n_y = width["gy"]
    exchanges = 2 + 2 * SWEEPS
    box = (E, E * E)
    field = pltpu.VMEM((E * E, L), jnp.float32)
    padded = pltpu.VMEM(((E + 2) * E, L), jnp.float32)
    faces = pltpu.VMEM((exchanges, 6, E, L), jnp.float32)
    own = pltpu.VMEM((PER,) + box, jnp.float32)
    moved = pltpu.VMEM((n_y - 1,) + box, jnp.float32)
    half = pltpu.VMEM((n_y - 1, E // 2, E * E), jnp.float32)
    out = jax.ShapeDtypeStruct((E, E, L), jnp.float32)
    return pl.pallas_call(
        functools.partial(kernel, width),
        out_shape=(out, out),
        in_specs=[pl.BlockSpec(memory_space=pltpu.SMEM)]
        + [pl.BlockSpec(memory_space=pl.ANY)] * 4,
        out_specs=(pl.BlockSpec(memory_space=pltpu.VMEM),) * 2,
        scratch_shapes=[own] * 4
        + [moved, half, moved, moved] * 2
        + [padded, padded]
        + [field] * 6
        + [pltpu.VMEM(((E + 1) * E, L), jnp.float32)]
        + [field] * 2
        + [faces] * 2
        + [
            pltpu.SemaphoreType.DMA((4,)),
            pltpu.SemaphoreType.DMA((4, n_y - 1)),
            pltpu.SemaphoreType.DMA((4, n_y - 1)),
            pltpu.SemaphoreType.DMA((exchanges, 6)),
            pltpu.SemaphoreType.DMA((exchanges, 6)),
        ],
        compiler_params=pltpu.CompilerParams(
            collective_id=0, has_side_effects=True, vmem_limit_bytes=40 * 1024 * 1024
        ),
        cost_estimate=pl.CostEstimate(
            flops=100 * E * E * L, bytes_accessed=24 * E * E * L, transcendentals=0
        ),
    )(corners, solution_old, right_side, acoef, bcoef)


def solution(mesh):
    width = dict(mesh.shape)
    boxes = P(("gx", "gy", "gz"), None, None)
    level = P("gx", "gy", "gz")
    return jax.shard_map(
        functools.partial(per_device, width),
        mesh=mesh,
        in_specs=(boxes, boxes, boxes, boxes, P()),
        out_specs=(level, level),
        check_vma=False,
    )
```

```python
import functools

import jax
import jax.numpy as jnp
from jax import lax
from jax.experimental import pallas as pl
from jax.experimental.pallas import tpu as pltpu
from jax.sharding import PartitionSpec as P

SWEEPS = 2
E = 32
L = 128
PER = 4
ST = E + 8
MESH = pl.DeviceIdType.MESH
SIDES = (("gx", -1), ("gx", 1), ("gy", -1), ("gy", 1), ("gz", -1), ("gz", 1))


def kernel(
    width,
    corners,
    sol_in,
    rhs_in,
    abs_in,
    dif_in,
    sol_out,
    res_out,
    own_b,
    own_u,
    own_a,
    own_f,
    st_b,
    st_u,
    st_a,
    st_f,
    rv_b,
    rv_u,
    rv_a,
    rv_f,
    b,
    u,
    f,
    dia,
    inv,
    res,
    cxl,
    cxh,
    cy,
    czl,
    czh,
    ez,
    ezi,
    hs,
    hr,
    in_sem,
    ms_sem,
    mr_sem,
    hs_sem,
    hr_sem,
):
    me = {axis: lax.axis_index(axis) for axis in ("gx", "gy", "gz")}
    n_y = width["gy"]
    my_y = me["gy"]

    loads = [
        pltpu.make_async_copy(src, dst, in_sem.at[i])
        for i, (src, dst) in enumerate(
            ((dif_in, own_b), (sol_in, own_u), (abs_in, own_a), (rhs_in, own_f))
        )
    ]
    for load in loads:
        load.start()

    def exists(side):
        axis, step = SIDES[side]
        return me[axis] > 0 if step < 0 else me[axis] < width[axis] - 1

    hr[...] = jnp.zeros_like(hr)
    b[...] = jnp.zeros_like(b)
    u[...] = jnp.zeros_like(u)

    barrier = pltpu.get_barrier_semaphore()
    partners = n_y - 1
    for k in range(1, n_y):
        pl.semaphore_signal(
            barrier, inc=1, device_id={"gy": lax.rem(my_y + k, n_y)}, device_id_type=MESH
        )
    for side in (0, 1, 4, 5):
        axis, step = SIDES[side]

        @pl.when(exists(side))
        def _():
            pl.semaphore_signal(
                barrier, inc=1, device_id={axis: me[axis] + step}, device_id_type=MESH
            )

        partners = partners + exists(side).astype(jnp.int32)

    def owner_inner(device, slot):
        row = ((me["gx"] * n_y + device) * width["gz"] + me["gz"]) * PER + slot
        return lax.div(corners[1, row], E), lax.div(lax.rem(corners[2, row], PER * E), E)

    mine = [owner_inner(my_y, s) for s in range(PER)]
    send_slot = []
    for k in range(1, n_y):
        target = lax.rem(my_y + k, n_y)
        slot = jnp.int32(0)
        for s in range(PER):
            slot = jnp.where(mine[s][0] == target, s, slot)
        send_slot.append(slot)
    own_slot = [jnp.int32(0)] * PER
    is_own = [jnp.int32(0)] * PER
    got_slot = [jnp.int32(0)] * PER
    for q in range(PER):
        for s in range(PER):
            here = (mine[s][0] == my_y) & (mine[s][1] == q)
            own_slot[q] = jnp.where(here, s, own_slot[q])
            is_own[q] = jnp.where(here, 1, is_own[q])
    for k in range(1, n_y):
        device = lax.rem(my_y + n_y - k, n_y)
        for s in range(PER):
            owner, inner = owner_inner(device, s)
            for q in range(PER):
                got_slot[q] = jnp.where((owner == my_y) & (inner == q), k - 1, got_slot[q])

    row = lax.broadcasted_iota(jnp.int32, (E, L), 0)
    lane = lax.broadcasted_iota(jnp.int32, (E, L), 1)
    wide_row = lax.broadcasted_iota(jnp.int32, (E // 2, E * E), 0)
    wide_lane = lax.broadcasted_iota(jnp.int32, (E // 2, E * E), 1)
    odd_half = (wide_row + wide_lane // E + wide_lane) % 2 == 1

    def migrate(i, k, st, rv):
        return pltpu.make_async_remote_copy(
            src_ref=st.at[k - 1],
            dst_ref=rv.at[k - 1],
            send_sem=ms_sem.at[i, k - 1],
            recv_sem=mr_sem.at[i, k - 1],
            device_id={"gy": lax.rem(my_y + k, n_y)},
            device_id_type=MESH,
        )

    fields = ((own_b, st_b, rv_b), (own_u, st_u, rv_u), (own_a, st_a, rv_a), (own_f, st_f, rv_f))
    for i, (own, st, rv) in enumerate(fields):
        loads[i].wait()
        for k in range(1, n_y):
            box = own[send_slot[k - 1]]
            if i == 1:
                box = jnp.where(odd_half, box[: E // 2], pltpu.roll(box[E // 2 :], 1, 0))
            st[k - 1] = box
        if i == 0:
            pl.semaphore_wait(barrier, partners)
        for k in range(1, n_y):
            migrate(i, k, st, rv).start()

    def arrived(i):
        _, st, rv = fields[i]
        for k in range(1, n_y):
            migrate(i, k, st, rv).wait_recv()

    group = lane // E
    own_mask = [jnp.full((E, L), is_own[q], jnp.int32) == 1 for q in range(PER)]

    def assembled(i, put):
        own, _, rv = fields[i]

        def columns(t, carry):
            at = pl.ds(pl.multiple_of(t * L, L), L)
            parts = []
            for q in range(PER):
                got = rv[got_slot[q], :, at]
                if i == 1:
                    got = jnp.concatenate([got, pltpu.roll(got, E // 2 - 1, 0)], axis=0)
                parts.append(jnp.where(own_mask[q], own[own_slot[q], :, at], got))
            for j in range(PER):
                plane = parts[j]
                for q in range(PER):
                    if q != j:
                        plane = jnp.where(
                            group == q, pltpu.roll(parts[q], (q - j) * E % L, 1), plane
                        )
                put(t * PER + j, plane)
            return carry

        lax.fori_loop(0, E * E // L, columns, 0)

    def at_plane(y):
        return pl.ds(pl.multiple_of(y * E, E), E)

    def base(y):
        return pl.multiple_of(y * ST + ST + 8, 8)

    def padded(y):
        return pl.ds(base(y), E)

    even = (row + lane) % 2 == 0
    odd = (row + lane) % 2 == 1
    pair = lane // 2
    zero = jnp.zeros((E, L), jnp.float32)
    first = ST + 8

    def pack_z(y, v, face):
        return jnp.where(pair == y, pltpu.roll(v, 2 * y + 1, 1), face)

    def pack_all_z(ref):
        def planes(t, face):
            for j in range(4):
                y = t * 4 + j
                face = pack_z(y, ref[padded(y), :], face)
            return face

        return lax.fori_loop(0, E // 4, planes, zero)

    def z_halo(e):
        return jnp.where(lane % 2 == 0, hr[e, 4], pltpu.roll(hr[e, 5], L - 2, 1))

    def z_edge(halo, y):
        return pltpu.roll(halo, lax.rem(L - 2 * y, L), 1)

    def face_copy(e, side):
        axis, step = SIDES[side]
        return pltpu.make_async_remote_copy(
            src_ref=hs.at[e, side],
            dst_ref=hr.at[e, side ^ 1],
            send_sem=hs_sem.at[e, side],
            recv_sem=hr_sem.at[e, side ^ 1],
            device_id={axis: me[axis] + step},
            device_id_type=MESH,
        )

    def send_faces(e, ref, z_face):
        hs[e, 0] = ref[pl.ds(first, E, stride=ST), :]
        hs[e, 1] = ref[pl.ds(first + E - 1, E, stride=ST), :]
        hs[e, 2] = ref[pl.ds(first, E), :]
        hs[e, 3] = ref[pl.ds(first + (E - 1) * ST, E), :]
        hs[e, 4] = z_face
        hs[e, 5] = z_face
        for side in range(6):

            @pl.when(exists(side))
            def _():
                face_copy(e, side).start()

    def wait_faces(e):
        for side in range(6):
            axis, step = SIDES[side]

            @pl.when(exists(side))
            def _():
                pltpu.make_async_remote_copy(
                    src_ref=hs.at[e, side],
                    dst_ref=hr.at[e, side],
                    send_sem=hs_sem.at[e, side],
                    recv_sem=hr_sem.at[e, side],
                    device_id={axis: me[axis] + step},
                    device_id_type=MESH,
                ).wait_recv()

    arrived(0)

    def put_b(y, plane):
        b[padded(y), :] = plane

    assembled(0, put_b)
    send_faces(0, b, pack_all_z(b))

    arrived(1)

    def put_u(y, plane):
        u[padded(y), :] = plane

    assembled(1, put_u)
    send_faces(1, u, pack_all_z(u))

    wait_faces(0)
    b[pl.ds(first - 1, E, stride=ST), :] = hr[0, 0]
    b[pl.ds(first + E, E, stride=ST), :] = hr[0, 1]
    b[pl.ds(8, E), :] = hr[0, 2]
    b[pl.ds(first + E * ST, E), :] = hr[0, 3]
    b_halo = z_halo(0)

    def coefs(y, carry):
        v = b[padded(y), :]
        at = at_plane(y)
        edge = z_edge(b_halo, y)
        x_low = 0.5 * (b[pl.ds(base(y) - 1, E), :] + v)
        x_high = 0.5 * (b[pl.ds(base(y) + 1, E), :] + v)
        y_low = 0.5 * (b[padded(y - 1), :] + v)
        y_high = 0.5 * (b[padded(y + 1), :] + v)
        z_low = 0.5 * (jnp.where(lane == 0, edge, pltpu.roll(v, 1, 1)) + v)
        z_high = 0.5 * (jnp.where(lane == L - 1, edge, pltpu.roll(v, L - 1, 1)) + v)
        cxl[at, :] = x_low
        cxh[at, :] = x_high
        cy[at, :] = y_low
        cy[at_plane(y + 1), :] = y_high
        czl[at, :] = jnp.where(lane == 0, 0.0, z_low)
        czh[at, :] = jnp.where(lane == L - 1, 0.0, z_high)
        ez[at, :] = jnp.where(lane == 0, z_low, jnp.where(lane == L - 1, z_high, 0.0))
        dia[at, :] = (x_high + x_low) + (y_high + y_low) + (z_high + z_low)
        return carry

    lax.fori_loop(0, E, coefs, 0)

    arrived(2)

    def put_a(y, plane):
        at = at_plane(y)
        total = plane + dia[at, :]
        inverse = 1.0 / total
        dia[at, :] = total
        inv[at, :] = inverse
        ezi[at, :] = ez[at, :] * inverse

    assembled(2, put_a)
    arrived(3)

    def put_f(y, plane):
        f[at_plane(y), :] = plane

    assembled(3, put_f)

    def neighbours(y):
        at = at_plane(y)
        v = u[padded(y), :]
        x_sum = cxh[at, :] * u[pl.ds(base(y) + 1, E), :] + cxl[at, :] * u[pl.ds(base(y) - 1, E), :]
        y_sum = cy[at_plane(y + 1), :] * u[padded(y + 1), :] + cy[at, :] * u[padded(y - 1), :]
        z_sum = czh[at, :] * pltpu.roll(v, L - 1, 1) + czl[at, :] * pltpu.roll(v, 1, 1)
        return v, x_sum + y_sum + z_sum

    low_x = pl.ds(0, E, stride=E)
    high_x = pl.ds(E - 1, E, stride=E)
    low_y = pl.ds(0, E)
    high_y = pl.ds((E - 1) * E, E)
    top_y = pl.ds(E * E, E)

    e = 1
    for sweep in range(SWEEPS):
        for colour in (0, 1):
            masks = (even, odd) if colour == 0 else (odd, even)

            def planes(t, carry):
                for j in range(4):
                    y = t * 4 + j
                    at = at_plane(y)
                    v, total = neighbours(y)
                    new = (f[at, :] + total) * inv[at, :]
                    u[padded(y), :] = jnp.where(masks[j % 2], new, v)
                return carry

            lax.fori_loop(0, E // 4, planes, 0)
            wait_faces(e)
            for at, mask, term in (
                (pl.ds(first, E, stride=ST), 0, cxl[low_x, :] * inv[low_x, :] * hr[e, 0]),
                (pl.ds(first + E - 1, E, stride=ST), 1, cxh[high_x, :] * inv[high_x, :] * hr[e, 1]),
                (pl.ds(first, E), 0, cy[low_y, :] * inv[low_y, :] * hr[e, 2]),
                (pl.ds(first + (E - 1) * ST, E), 1, cy[top_y, :] * inv[high_y, :] * hr[e, 3]),
            ):
                u[at, :] = u[at, :] + jnp.where(masks[mask], term, 0.0)
            halo = z_halo(e)

            def edges(t, face):
                for j in range(4):
                    y = t * 4 + j
                    term = ezi[at_plane(y), :] * z_edge(halo, y)
                    v = u[padded(y), :] + jnp.where(masks[j % 2], term, 0.0)
                    u[padded(y), :] = v
                    face = pack_z(y, v, face)
                return face

            face = lax.fori_loop(0, E // 4, edges, zero)
            e += 1
            send_faces(e, u, face)

    def residual(t, carry):
        for j in range(4):
            y = t * 4 + j
            at = at_plane(y)
            v, total = neighbours(y)
            res[at, :] = f[at, :] - (dia[at, :] * v - total)
        return carry

    lax.fori_loop(0, E // 4, residual, 0)
    for x in range(E):
        sol_out[x] = u[pl.ds(first + x, E, stride=ST), :]
    wait_faces(e)
    for at, term in (
        (low_x, cxl[low_x, :] * hr[e, 0]),
        (high_x, cxh[high_x, :] * hr[e, 1]),
        (low_y, cy[low_y, :] * hr[e, 2]),
        (high_y, cy[top_y, :] * hr[e, 3]),
    ):
        res[at, :] = res[at, :] + term
    last_halo = z_halo(e)

    def last_edges(t, carry):
        for j in range(4):
            y = t * 4 + j
            at = at_plane(y)
            res[at, :] = res[at, :] + ez[at, :] * z_edge(last_halo, y)
        return carry

    lax.fori_loop(0, E // 4, last_edges, 0)
    for x in range(E):
        res_out[x] = res[pl.ds(x, E, stride=E), :]

    for i, (_, st, rv) in enumerate(fields):
        for k in range(1, n_y):
            migrate(i, k, st, rv).wait_send()
    for exchange in range(e + 1):
        for side in range(6):

            @pl.when(exists(side))
            def _():
                face_copy(exchange, side).wait_send()


def per_device(width, solution_old, right_side, acoef, bcoef, corners):
    n_y = width["gy"]
    exchanges = 2 + 2 * SWEEPS
    box = (E, E * E)
    field = pltpu.VMEM((E * E, L), jnp.float32)
    padded = pltpu.VMEM(((E + 2) * ST + 16, L), jnp.float32)
    faces = pltpu.VMEM((exchanges, 6, E, L), jnp.float32)
    own = pltpu.VMEM((PER,) + box, jnp.float32)
    moved = pltpu.VMEM((n_y - 1,) + box, jnp.float32)
    half = pltpu.VMEM((n_y - 1, E // 2, E * E), jnp.float32)
    out = jax.ShapeDtypeStruct((E, E, L), jnp.float32)
    return pl.pallas_call(
        functools.partial(kernel, width),
        out_shape=(out, out),
        in_specs=[pl.BlockSpec(memory_space=pltpu.SMEM)]
        + [pl.BlockSpec(memory_space=pl.ANY)] * 4,
        out_specs=(pl.BlockSpec(memory_space=pltpu.VMEM),) * 2,
        scratch_shapes=[own] * 4
        + [moved, half, moved, moved] * 2
        + [padded, padded]
        + [field] * 6
        + [pltpu.VMEM(((E + 1) * E, L), jnp.float32)]
        + [field] * 4
        + [faces] * 2
        + [
            pltpu.SemaphoreType.DMA((4,)),
            pltpu.SemaphoreType.DMA((4, n_y - 1)),
            pltpu.SemaphoreType.DMA((4, n_y - 1)),
            pltpu.SemaphoreType.DMA((exchanges, 6)),
            pltpu.SemaphoreType.DMA((exchanges, 6)),
        ],
        compiler_params=pltpu.CompilerParams(
            collective_id=0, has_side_effects=True, vmem_limit_bytes=64 * 1024 * 1024
        ),
        cost_estimate=pl.CostEstimate(
            flops=100 * E * E * L, bytes_accessed=24 * E * E * L, transcendentals=0
        ),
    )(corners, solution_old, right_side, acoef, bcoef)


def solution(mesh):
    width = dict(mesh.shape)
    boxes = P(("gx", "gy", "gz"), None, None)
    level = P("gx", "gy", "gz")
    return jax.shard_map(
        functools.partial(per_device, width),
        mesh=mesh,
        in_specs=(boxes, boxes, boxes, boxes, P()),
        out_specs=(level, level),
        check_vma=False,
    )
```

```python
import functools

import jax
import jax.numpy as jnp
from jax import lax
from jax.experimental import pallas as pl
from jax.experimental.pallas import tpu as pltpu
from jax.sharding import PartitionSpec as P

SWEEPS = 2
E = 32
L = 128
PER = 4
ST = E + 8
MESH = pl.DeviceIdType.MESH
SIDES = (("gx", -1), ("gx", 1), ("gy", -1), ("gy", 1), ("gz", -1), ("gz", 1))


def kernel(
    width,
    corners,
    sol_in,
    rhs_in,
    abs_in,
    dif_in,
    sol_out,
    res_out,
    own_b,
    own_u,
    own_a,
    own_f,
    st_b,
    st_u,
    st_a,
    st_f,
    rv_b,
    rv_u,
    rv_a,
    rv_f,
    b,
    u,
    f,
    dia,
    inv,
    res,
    cxl,
    cxh,
    cy,
    czl,
    czh,
    ez,
    ezi,
    hs,
    hr,
    in_sem,
    ms_sem,
    mr_sem,
    hs_sem,
    hr_sem,
):
    me = {axis: lax.axis_index(axis) for axis in ("gx", "gy", "gz")}
    n_y = width["gy"]
    my_y = me["gy"]

    loads = [
        pltpu.make_async_copy(src, dst, in_sem.at[i])
        for i, (src, dst) in enumerate(
            ((dif_in, own_b), (sol_in, own_u), (abs_in, own_a), (rhs_in, own_f))
        )
    ]
    for load in loads:
        load.start()

    def exists(side):
        axis, step = SIDES[side]
        return me[axis] > 0 if step < 0 else me[axis] < width[axis] - 1

    hr[...] = jnp.zeros_like(hr)
    b[...] = jnp.zeros_like(b)
    u[...] = jnp.zeros_like(u)

    barrier = pltpu.get_barrier_semaphore()
    partners = 0
    for side in range(6):
        axis, step = SIDES[side]

        @pl.when(exists(side))
        def _():
            pl.semaphore_signal(
                barrier, inc=1, device_id={axis: me[axis] + step}, device_id_type=MESH
            )

        partners = partners + exists(side).astype(jnp.int32)

    def owner_inner(device, slot):
        row = ((me["gx"] * n_y + device) * width["gz"] + me["gz"]) * PER + slot
        return lax.div(corners[1, row], E), lax.div(lax.rem(corners[2, row], PER * E), E)

    table = [[owner_inner(j, s) for s in range(PER)] for j in range(n_y)]
    goes, its_slot, its_inner = {}, {}, {}
    for j in range(n_y):
        for t in range(n_y):
            if t != j:
                live, slot, inner = jnp.int32(0), jnp.int32(0), jnp.int32(0)
                for s in range(PER):
                    hit = table[j][s][0] == t
                    live = jnp.where(hit, 1, live)
                    slot = jnp.where(hit, s, slot)
                    inner = jnp.where(hit, table[j][s][1], inner)
                goes[j, t], its_slot[j, t], its_inner[j, t] = live, slot, inner

    n_slot = n_y - 1
    rank = {}
    code = [[jnp.int32(0)] * n_slot for _ in range(2)]
    for way in range(2):
        for c in range(n_y):
            at = (lambda i: i) if way == 0 else (lambda i: n_y - 1 - i)
            here = [jnp.int32(0)] * n_slot
            count = jnp.int32(0)
            for t in range(n_y - 1, c, -1):
                for j in range(c + 1):
                    pair = (at(j), at(t))
                    rank[way, c, j, t] = count
                    held = its_slot[pair] if j == c else PER + rank[way, c - 1, j, t]
                    for k in range(n_slot):
                        here[k] = jnp.where((goes[pair] == 1) & (count == k), held, here[k])
                    count = count + goes[pair]
            for k in range(n_slot):
                code[way][k] = jnp.where(my_y == at(c), here[k], code[way][k])

    inward = jnp.where(my_y < n_y // 2, 0, 1)
    outward = 1 - inward

    row = lax.broadcasted_iota(jnp.int32, (E, L), 0)
    lane = lax.broadcasted_iota(jnp.int32, (E, L), 1)
    wide_row = lax.broadcasted_iota(jnp.int32, (E // 2, E * E), 0)
    wide_lane = lax.broadcasted_iota(jnp.int32, (E // 2, E * E), 1)
    odd_half = (wide_row + wide_lane // E + wide_lane) % 2 == 1

    fields = ((own_b, st_b, rv_b), (own_u, st_u, rv_u), (own_a, st_a, rv_a), (own_f, st_f, rv_f))
    chunks = (4, 1, 2, 2)

    def part_of(ref, i, way, part):
        if part == chunks[i]:
            return ref.at[way, n_slot - 1]
        rows = ref.shape[2] // chunks[i]
        return ref.at[way, pl.ds(0, n_slot - 1), pl.ds(part * rows, rows)]

    def hop(i, way, part, neighbour):
        _, st, rv = fields[i]
        return pltpu.make_async_remote_copy(
            src_ref=part_of(st, i, way, part),
            dst_ref=part_of(rv, i, way, part),
            send_sem=ms_sem.at[i, way, part],
            recv_sem=mr_sem.at[i, way, part],
            device_id={"gy": neighbour},
            device_id_type=MESH,
        )

    def sends(way):
        return jnp.where(way == 0, my_y < n_y - 1, my_y > 0)

    def receives(way):
        return jnp.where(way == 0, my_y > 0, my_y < n_y - 1)

    def fill(i, way, k, start, rows):
        own, st, rv = fields[i]
        held = jnp.where(way == 0, code[0][k], code[1][k])
        slot = jnp.where(held < PER, held, 0)
        if i == 1:
            box = own[slot]
            box = jnp.where(odd_half, box[: E // 2], pltpu.roll(box[E // 2 :], 1, 0))
        else:
            box = own[slot, pl.ds(start, rows), :]
        for r in range(n_slot - 1):
            relayed = jnp.full((rows, E * E), held, jnp.int32) == PER + r
            box = jnp.where(relayed, rv[way, r, pl.ds(start, rows), :], box)
        st[way, k, pl.ds(start, rows), :] = box

    def take_hop(i, way, part):
        @pl.when(receives(way))
        def _():
            hop(i, way, part, my_y - 1 + 2 * way).wait_recv()

    def pass_on(i, way, part):
        rows = fields[i][1].shape[2]
        if part < chunks[i]:
            take_hop(i, way, part)
            rows = rows // chunks[i]
            for k in range(n_slot - 1):
                fill(i, way, k, part * rows, rows)
        else:
            fill(i, way, n_slot - 1, 0, rows)

        @pl.when(sends(way))
        def _():
            hop(i, way, part, my_y + 1 - 2 * way).start()

    steps = [(i, part) for i in range(4) for part in range(chunks[i] + 1)]
    lag = 2

    def migrate(first_step, last_step):
        for n in range(first_step, last_step):
            if n < len(steps):
                i, part = steps[n]
                if part == 0:
                    loads[i].wait()
                if n == 0:
                    pl.semaphore_wait(barrier, partners)
                pass_on(i, inward, part)
            if 0 <= n - lag < len(steps):
                pass_on(steps[n - lag][0], outward, steps[n - lag][1])

    def arrived(i):
        for way in range(2):
            take_hop(i, way, chunks[i])

    migrate(0, 9)

    own_slot = [jnp.int32(0)] * PER
    is_own = [jnp.int32(0)] * PER
    got_slot = [jnp.int32(0)] * PER
    got_way = [jnp.int32(0)] * PER
    for q in range(PER):
        for s in range(PER):
            owner, inner = owner_inner(my_y, s)
            here = (owner == my_y) & (inner == q)
            own_slot[q] = jnp.where(here, s, own_slot[q])
            is_own[q] = jnp.where(here, 1, is_own[q])
        for way in range(2):
            for t in range(1, n_y):
                for j in range(t):
                    pair = (j, t) if way == 0 else (n_y - 1 - j, n_y - 1 - t)
                    here = (goes[pair] == 1) & (its_inner[pair] == q) & (my_y == pair[1])
                    slot = jnp.minimum(rank[way, t - 1, j, t], n_slot - 1)
                    got_slot[q] = jnp.where(here, slot, got_slot[q])
                    got_way[q] = jnp.where(here, way, got_way[q])

    group = lane // E
    own_mask = [jnp.full((E, L), is_own[q], jnp.int32) == 1 for q in range(PER)]

    def assembled(i, put):
        own, _, rv = fields[i]

        def columns(t, carry):
            at = pl.ds(pl.multiple_of(t * L, L), L)
            parts = []
            for q in range(PER):
                got = rv[got_way[q], got_slot[q], :, at]
                if i == 1:
                    got = jnp.concatenate([got, pltpu.roll(got, E // 2 - 1, 0)], axis=0)
                parts.append(jnp.where(own_mask[q], own[own_slot[q], :, at], got))
            for j in range(PER):
                plane = parts[j]
                for q in range(PER):
                    if q != j:
                        plane = jnp.where(
                            group == q, pltpu.roll(parts[q], (q - j) * E % L, 1), plane
                        )
                put(t * PER + j, plane)
            return carry

        lax.fori_loop(0, E * E // L, columns, 0)

    def at_plane(y):
        return pl.ds(pl.multiple_of(y * E, E), E)

    def base(y):
        return pl.multiple_of(y * ST + ST + 8, 8)

    def padded(y):
        return pl.ds(base(y), E)

    even = (row + lane) % 2 == 0
    odd = (row + lane) % 2 == 1
    pair = lane // 2
    zero = jnp.zeros((E, L), jnp.float32)
    first = ST + 8

    def pack_z(y, v, face):
        return jnp.where(pair == y, pltpu.roll(v, 2 * y + 1, 1), face)

    def pack_all_z(ref):
        def planes(t, face):
            for j in range(4):
                y = t * 4 + j
                face = pack_z(y, ref[padded(y), :], face)
            return face

        return lax.fori_loop(0, E // 4, planes, zero)

    def z_halo(e):
        return jnp.where(lane % 2 == 0, hr[e, 4], pltpu.roll(hr[e, 5], L - 2, 1))

    def z_edge(halo, y):
        return pltpu.roll(halo, lax.rem(L - 2 * y, L), 1)

    def face_copy(e, side):
        axis, step = SIDES[side]
        return pltpu.make_async_remote_copy(
            src_ref=hs.at[e, side],
            dst_ref=hr.at[e, side ^ 1],
            send_sem=hs_sem.at[e, side],
            recv_sem=hr_sem.at[e, side ^ 1],
            device_id={axis: me[axis] + step},
            device_id_type=MESH,
        )

    def send_faces(e, ref, z_face):
        hs[e, 0] = ref[pl.ds(first, E, stride=ST), :]
        hs[e, 1] = ref[pl.ds(first + E - 1, E, stride=ST), :]
        hs[e, 2] = ref[pl.ds(first, E), :]
        hs[e, 3] = ref[pl.ds(first + (E - 1) * ST, E), :]
        hs[e, 4] = z_face
        hs[e, 5] = z_face
        for side in range(6):

            @pl.when(exists(side))
            def _():
                face_copy(e, side).start()

    def wait_faces(e):
        for side in range(6):
            axis, step = SIDES[side]

            @pl.when(exists(side))
            def _():
                pltpu.make_async_remote_copy(
                    src_ref=hs.at[e, side],
                    dst_ref=hr.at[e, side],
                    send_sem=hs_sem.at[e, side],
                    recv_sem=hr_sem.at[e, side],
                    device_id={axis: me[axis] + step},
                    device_id_type=MESH,
                ).wait_recv()

    arrived(0)

    def put_b(y, plane):
        b[padded(y), :] = plane

    assembled(0, put_b)
    send_faces(0, b, pack_all_z(b))

    arrived(1)

    def put_u(y, plane):
        u[padded(y), :] = plane

    assembled(1, put_u)
    send_faces(1, u, pack_all_z(u))

    migrate(9, 11)
    wait_faces(0)
    b[pl.ds(first - 1, E, stride=ST), :] = hr[0, 0]
    b[pl.ds(first + E, E, stride=ST), :] = hr[0, 1]
    b[pl.ds(8, E), :] = hr[0, 2]
    b[pl.ds(first + E * ST, E), :] = hr[0, 3]
    b_halo = z_halo(0)

    def coefs(y, carry):
        v = b[padded(y), :]
        at = at_plane(y)
        edge = z_edge(b_halo, y)
        x_low = 0.5 * (b[pl.ds(base(y) - 1, E), :] + v)
        x_high = 0.5 * (b[pl.ds(base(y) + 1, E), :] + v)
        y_low = 0.5 * (b[padded(y - 1), :] + v)
        y_high = 0.5 * (b[padded(y + 1), :] + v)
        z_low = 0.5 * (jnp.where(lane == 0, edge, pltpu.roll(v, 1, 1)) + v)
        z_high = 0.5 * (jnp.where(lane == L - 1, edge, pltpu.roll(v, L - 1, 1)) + v)
        cxl[at, :] = x_low
        cxh[at, :] = x_high
        cy[at, :] = y_low
        cy[at_plane(y + 1), :] = y_high
        czl[at, :] = jnp.where(lane == 0, 0.0, z_low)
        czh[at, :] = jnp.where(lane == L - 1, 0.0, z_high)
        ez[at, :] = jnp.where(lane == 0, z_low, jnp.where(lane == L - 1, z_high, 0.0))
        dia[at, :] = (x_high + x_low) + (y_high + y_low) + (z_high + z_low)
        return carry

    lax.fori_loop(0, E, coefs, 0)

    migrate(11, len(steps) + lag)
    arrived(2)

    def put_a(y, plane):
        at = at_plane(y)
        total = plane + dia[at, :]
        inverse = 1.0 / total
        dia[at, :] = total
        inv[at, :] = inverse
        ezi[at, :] = ez[at, :] * inverse

    assembled(2, put_a)
    arrived(3)

    def put_f(y, plane):
        f[at_plane(y), :] = plane

    assembled(3, put_f)

    def neighbours(y):
        at = at_plane(y)
        v = u[padded(y), :]
        x_sum = cxh[at, :] * u[pl.ds(base(y) + 1, E), :] + cxl[at, :] * u[pl.ds(base(y) - 1, E), :]
        y_sum = cy[at_plane(y + 1), :] * u[padded(y + 1), :] + cy[at, :] * u[padded(y - 1), :]
        z_sum = czh[at, :] * pltpu.roll(v, L - 1, 1) + czl[at, :] * pltpu.roll(v, 1, 1)
        return v, x_sum + y_sum + z_sum

    low_x = pl.ds(0, E, stride=E)
    high_x = pl.ds(E - 1, E, stride=E)
    low_y = pl.ds(0, E)
    high_y = pl.ds((E - 1) * E, E)
    top_y = pl.ds(E * E, E)

    e = 1
    for sweep in range(SWEEPS):
        for colour in (0, 1):
            masks = (even, odd) if colour == 0 else (odd, even)

            def planes(t, carry):
                for j in range(4):
                    y = t * 4 + j
                    at = at_plane(y)
                    v, total = neighbours(y)
                    new = (f[at, :] + total) * inv[at, :]
                    u[padded(y), :] = jnp.where(masks[j % 2], new, v)
                return carry

            lax.fori_loop(0, E // 4, planes, 0)
            wait_faces(e)
            for at, mask, term in (
                (pl.ds(first, E, stride=ST), 0, cxl[low_x, :] * inv[low_x, :] * hr[e, 0]),
                (pl.ds(first + E - 1, E, stride=ST), 1, cxh[high_x, :] * inv[high_x, :] * hr[e, 1]),
                (pl.ds(first, E), 0, cy[low_y, :] * inv[low_y, :] * hr[e, 2]),
                (pl.ds(first + (E - 1) * ST, E), 1, cy[top_y, :] * inv[high_y, :] * hr[e, 3]),
            ):
                u[at, :] = u[at, :] + jnp.where(masks[mask], term, 0.0)
            halo = z_halo(e)

            def edges(t, face):
                for j in range(4):
                    y = t * 4 + j
                    term = ezi[at_plane(y), :] * z_edge(halo, y)
                    v = u[padded(y), :] + jnp.where(masks[j % 2], term, 0.0)
                    u[padded(y), :] = v
                    face = pack_z(y, v, face)
                return face

            face = lax.fori_loop(0, E // 4, edges, zero)
            e += 1
            send_faces(e, u, face)

    def residual(t, carry):
        for j in range(4):
            y = t * 4 + j
            at = at_plane(y)
            v, total = neighbours(y)
            res[at, :] = f[at, :] - (dia[at, :] * v - total)
        return carry

    lax.fori_loop(0, E // 4, residual, 0)
    for x in range(E):
        sol_out[x] = u[pl.ds(first + x, E, stride=ST), :]
    wait_faces(e)
    for at, term in (
        (low_x, cxl[low_x, :] * hr[e, 0]),
        (high_x, cxh[high_x, :] * hr[e, 1]),
        (low_y, cy[low_y, :] * hr[e, 2]),
        (high_y, cy[top_y, :] * hr[e, 3]),
    ):
        res[at, :] = res[at, :] + term
    last_halo = z_halo(e)

    def last_edges(t, carry):
        for j in range(4):
            y = t * 4 + j
            at = at_plane(y)
            res[at, :] = res[at, :] + ez[at, :] * z_edge(last_halo, y)
        return carry

    lax.fori_loop(0, E // 4, last_edges, 0)
    for x in range(E):
        res_out[x] = res[pl.ds(x, E, stride=E), :]

    for i, part in steps:
        for way in range(2):

            @pl.when(sends(way))
            def _():
                hop(i, way, part, my_y + 1 - 2 * way).wait_send()

    for exchange in range(e + 1):
        for side in range(6):

            @pl.when(exists(side))
            def _():
                face_copy(exchange, side).wait_send()


def per_device(width, solution_old, right_side, acoef, bcoef, corners):
    n_y = width["gy"]
    exchanges = 2 + 2 * SWEEPS
    box = (E, E * E)
    field = pltpu.VMEM((E * E, L), jnp.float32)
    padded = pltpu.VMEM(((E + 2) * ST + 16, L), jnp.float32)
    faces = pltpu.VMEM((exchanges, 6, E, L), jnp.float32)
    own = pltpu.VMEM((PER,) + box, jnp.float32)
    moved = pltpu.VMEM((2, n_y - 1) + box, jnp.float32)
    half = pltpu.VMEM((2, n_y - 1, E // 2, E * E), jnp.float32)
    out = jax.ShapeDtypeStruct((E, E, L), jnp.float32)
    return pl.pallas_call(
        functools.partial(kernel, width),
        out_shape=(out, out),
        in_specs=[pl.BlockSpec(memory_space=pltpu.SMEM)]
        + [pl.BlockSpec(memory_space=pl.ANY)] * 4,
        out_specs=(pl.BlockSpec(memory_space=pltpu.VMEM),) * 2,
        scratch_shapes=[own] * 4
        + [moved, half, moved, moved] * 2
        + [padded, padded]
        + [field] * 6
        + [pltpu.VMEM(((E + 1) * E, L), jnp.float32)]
        + [field] * 4
        + [faces] * 2
        + [
            pltpu.SemaphoreType.DMA((4,)),
            pltpu.SemaphoreType.DMA((4, 2, 5)),
            pltpu.SemaphoreType.DMA((4, 2, 5)),
            pltpu.SemaphoreType.DMA((exchanges, 6)),
            pltpu.SemaphoreType.DMA((exchanges, 6)),
        ],
        compiler_params=pltpu.CompilerParams(
            collective_id=0, has_side_effects=True, vmem_limit_bytes=64 * 1024 * 1024
        ),
        cost_estimate=pl.CostEstimate(
            flops=100 * E * E * L, bytes_accessed=24 * E * E * L, transcendentals=0
        ),
    )(corners, solution_old, right_side, acoef, bcoef)


def solution(mesh):
    width = dict(mesh.shape)
    boxes = P(("gx", "gy", "gz"), None, None)
    level = P("gx", "gy", "gz")
    return jax.shard_map(
        functools.partial(per_device, width),
        mesh=mesh,
        in_specs=(boxes, boxes, boxes, boxes, P()),
        out_specs=(level, level),
        check_vma=False,
    )
```

```python
import functools

import jax
import jax.numpy as jnp
from jax import lax
from jax.experimental import pallas as pl
from jax.experimental.pallas import tpu as pltpu
from jax.sharding import PartitionSpec as P

SWEEPS = 2
E = 32
L = 128
PER = 4
ST = E + 8
MESH = pl.DeviceIdType.MESH
SIDES = (("gx", -1), ("gx", 1), ("gy", -1), ("gy", 1), ("gz", -1), ("gz", 1))


def kernel(
    width,
    corners,
    sol_in,
    rhs_in,
    abs_in,
    dif_in,
    sol_out,
    res_out,
    own_b,
    own_u,
    own_a,
    own_f,
    st_b,
    st_u,
    st_a,
    st_f,
    rv_b,
    rv_u,
    rv_a,
    rv_f,
    b,
    u,
    f,
    dia,
    inv,
    res,
    cxl,
    cxh,
    cy,
    czl,
    czh,
    ez,
    ezi,
    hs,
    hr,
    in_sem,
    ms_sem,
    mr_sem,
    hs_sem,
    hr_sem,
):
    me = {axis: lax.axis_index(axis) for axis in ("gx", "gy", "gz")}
    n_y = width["gy"]
    my_y = me["gy"]

    loads = [
        pltpu.make_async_copy(src, dst, in_sem.at[i])
        for i, (src, dst) in enumerate(
            ((dif_in, own_b), (sol_in, own_u), (abs_in, own_a), (rhs_in, own_f))
        )
    ]
    for load in loads:
        load.start()

    def exists(side):
        axis, step = SIDES[side]
        return me[axis] > 0 if step < 0 else me[axis] < width[axis] - 1

    hr[...] = jnp.zeros_like(hr)
    b[...] = jnp.zeros_like(b)
    u[...] = jnp.zeros_like(u)

    barrier = pltpu.get_barrier_semaphore()
    partners = 0
    for side in range(6):
        axis, step = SIDES[side]

        @pl.when(exists(side))
        def _():
            pl.semaphore_signal(
                barrier, inc=1, device_id={axis: me[axis] + step}, device_id_type=MESH
            )

        partners = partners + exists(side).astype(jnp.int32)

    def owner_inner(device, slot):
        row = ((me["gx"] * n_y + device) * width["gz"] + me["gz"]) * PER + slot
        return lax.div(corners[1, row], E), lax.div(lax.rem(corners[2, row], PER * E), E)

    table = [[owner_inner(j, s) for s in range(PER)] for j in range(n_y)]
    goes, its_slot, its_inner = {}, {}, {}
    for j in range(n_y):
        for t in range(n_y):
            if t != j:
                live, slot, inner = jnp.int32(0), jnp.int32(0), jnp.int32(0)
                for s in range(PER):
                    hit = table[j][s][0] == t
                    live = jnp.where(hit, 1, live)
                    slot = jnp.where(hit, s, slot)
                    inner = jnp.where(hit, table[j][s][1], inner)
                goes[j, t], its_slot[j, t], its_inner[j, t] = live, slot, inner

    n_slot = n_y - 1
    rank = {}
    code = [[jnp.int32(0)] * n_slot for _ in range(2)]
    for way in range(2):
        for c in range(n_y):
            at = (lambda i: i) if way == 0 else (lambda i: n_y - 1 - i)
            here = [jnp.int32(0)] * n_slot
            count = jnp.int32(0)
            for t in range(n_y - 1, c, -1):
                for j in range(c + 1):
                    pair = (at(j), at(t))
                    rank[way, c, j, t] = count
                    held = its_slot[pair] if j == c else PER + rank[way, c - 1, j, t]
                    for k in range(n_slot):
                        here[k] = jnp.where((goes[pair] == 1) & (count == k), held, here[k])
                    count = count + goes[pair]
            for k in range(n_slot):
                code[way][k] = jnp.where(my_y == at(c), here[k], code[way][k])

    inward = jnp.where(my_y < n_y // 2, 0, 1)
    outward = 1 - inward

    row = lax.broadcasted_iota(jnp.int32, (E, L), 0)
    lane = lax.broadcasted_iota(jnp.int32, (E, L), 1)
    wide_row = lax.broadcasted_iota(jnp.int32, (E // 2, E * E), 0)
    wide_lane = lax.broadcasted_iota(jnp.int32, (E // 2, E * E), 1)
    odd_half = (wide_row + wide_lane // E + wide_lane) % 2 == 1

    fields = ((own_b, st_b, rv_b), (own_u, st_u, rv_u), (own_a, st_a, rv_a), (own_f, st_f, rv_f))
    chunks = (4, 1, 2, 2)

    def part_of(ref, i, way, part):
        if part == chunks[i]:
            return ref.at[way, n_slot - 1]
        rows = ref.shape[2] // chunks[i]
        return ref.at[way, pl.ds(0, n_slot - 1), pl.ds(part * rows, rows)]

    def hop(i, way, part, neighbour):
        _, st, rv = fields[i]
        return pltpu.make_async_remote_copy(
            src_ref=part_of(st, i, way, part),
            dst_ref=part_of(rv, i, way, part),
            send_sem=ms_sem.at[i, way, part],
            recv_sem=mr_sem.at[i, way, part],
            device_id={"gy": neighbour},
            device_id_type=MESH,
        )

    def sends(way):
        return jnp.where(way == 0, my_y < n_y - 1, my_y > 0)

    def receives(way):
        return jnp.where(way == 0, my_y > 0, my_y < n_y - 1)

    def fill(i, way, k, start, rows):
        own, st, rv = fields[i]
        held = jnp.where(way == 0, code[0][k], code[1][k])
        slot = jnp.where(held < PER, held, 0)
        if i == 1:
            box = own[slot]
            box = jnp.where(odd_half, box[: E // 2], pltpu.roll(box[E // 2 :], 1, 0))
        else:
            box = own[slot, pl.ds(start, rows), :]
        for r in range(n_slot - 1):
            relayed = jnp.full((rows, E * E), held, jnp.int32) == PER + r
            box = jnp.where(relayed, rv[way, r, pl.ds(start, rows), :], box)
        st[way, k, pl.ds(start, rows), :] = box

    def take_hop(i, way, part):
        @pl.when(receives(way))
        def _():
            hop(i, way, part, my_y - 1 + 2 * way).wait_recv()

    def pass_on(i, way, part):
        @pl.when(sends(way))
        def _():
            rows = fields[i][1].shape[2]
            if part < chunks[i]:
                take_hop(i, way, part)
                rows = rows // chunks[i]
                for k in range(n_slot - 1):
                    fill(i, way, k, part * rows, rows)
            else:
                fill(i, way, n_slot - 1, 0, rows)
            hop(i, way, part, my_y + 1 - 2 * way).start()

    steps = [(i, part) for i in range(4) for part in range(chunks[i] + 1)]
    lag = 3

    def migrate(first_step, last_step):
        for n in range(first_step, last_step):
            if n < len(steps):
                i, part = steps[n]
                if part == 0:
                    loads[i].wait()
                if n == 0:
                    pl.semaphore_wait(barrier, partners)
                pass_on(i, inward, part)
            if 0 <= n - lag < len(steps):
                pass_on(steps[n - lag][0], outward, steps[n - lag][1])

    def arrived(i):
        for way in range(2):

            @pl.when(jnp.logical_not(sends(way)))
            def _():
                for part in range(chunks[i]):
                    take_hop(i, way, part)

            take_hop(i, way, chunks[i])

    migrate(0, 9)

    own_slot = [jnp.int32(0)] * PER
    is_own = [jnp.int32(0)] * PER
    got_slot = [jnp.int32(0)] * PER
    got_way = [jnp.int32(0)] * PER
    for q in range(PER):
        for s in range(PER):
            owner, inner = owner_inner(my_y, s)
            here = (owner == my_y) & (inner == q)
            own_slot[q] = jnp.where(here, s, own_slot[q])
            is_own[q] = jnp.where(here, 1, is_own[q])
        for way in range(2):
            for t in range(1, n_y):
                for j in range(t):
                    pair = (j, t) if way == 0 else (n_y - 1 - j, n_y - 1 - t)
                    here = (goes[pair] == 1) & (its_inner[pair] == q) & (my_y == pair[1])
                    slot = jnp.minimum(rank[way, t - 1, j, t], n_slot - 1)
                    got_slot[q] = jnp.where(here, slot, got_slot[q])
                    got_way[q] = jnp.where(here, way, got_way[q])

    group = lane // E
    own_mask = [jnp.full((E, L), is_own[q], jnp.int32) == 1 for q in range(PER)]

    def assembled(i, put):
        own, _, rv = fields[i]

        def columns(t, carry):
            at = pl.ds(pl.multiple_of(t * L, L), L)
            parts = []
            for q in range(PER):
                got = rv[got_way[q], got_slot[q], :, at]
                if i == 1:
                    got = jnp.concatenate([got, pltpu.roll(got, E // 2 - 1, 0)], axis=0)
                parts.append(jnp.where(own_mask[q], own[own_slot[q], :, at], got))
            for j in range(PER):
                plane = parts[j]
                for q in range(PER):
                    if q != j:
                        plane = jnp.where(
                            group == q, pltpu.roll(parts[q], (q - j) * E % L, 1), plane
                        )
                put(t * PER + j, plane)
            return carry

        lax.fori_loop(0, E * E // L, columns, 0)

    def at_plane(y):
        return pl.ds(pl.multiple_of(y * E, E), E)

    def base(y):
        return pl.multiple_of(y * ST + ST + 8, 8)

    def padded(y):
        return pl.ds(base(y), E)

    even = (row + lane) % 2 == 0
    odd = (row + lane) % 2 == 1
    pair = lane // 2
    zero = jnp.zeros((E, L), jnp.float32)
    first = ST + 8

    def pack_z(y, v, face):
        return jnp.where(pair == y, pltpu.roll(v, 2 * y + 1, 1), face)

    def pack_all_z(ref):
        def planes(t, face):
            for j in range(4):
                y = t * 4 + j
                face = pack_z(y, ref[padded(y), :], face)
            return face

        return lax.fori_loop(0, E // 4, planes, zero)

    def z_halo(e):
        return jnp.where(lane % 2 == 0, hr[e, 4], pltpu.roll(hr[e, 5], L - 2, 1))

    def z_edge(halo, y):
        return pltpu.roll(halo, lax.rem(L - 2 * y, L), 1)

    def face_copy(e, side):
        axis, step = SIDES[side]
        return pltpu.make_async_remote_copy(
            src_ref=hs.at[e, side],
            dst_ref=hr.at[e, side ^ 1],
            send_sem=hs_sem.at[e, side],
            recv_sem=hr_sem.at[e, side ^ 1],
            device_id={axis: me[axis] + step},
            device_id_type=MESH,
        )

    def send_faces(e, ref, z_face):
        hs[e, 0] = ref[pl.ds(first, E, stride=ST), :]
        hs[e, 1] = ref[pl.ds(first + E - 1, E, stride=ST), :]
        hs[e, 2] = ref[pl.ds(first, E), :]
        hs[e, 3] = ref[pl.ds(first + (E - 1) * ST, E), :]
        hs[e, 4] = z_face
        hs[e, 5] = z_face
        for side in range(6):

            @pl.when(exists(side))
            def _():
                face_copy(e, side).start()

    def wait_faces(e):
        for side in range(6):
            axis, step = SIDES[side]

            @pl.when(exists(side))
            def _():
                pltpu.make_async_remote_copy(
                    src_ref=hs.at[e, side],
                    dst_ref=hr.at[e, side],
                    send_sem=hs_sem.at[e, side],
                    recv_sem=hr_sem.at[e, side],
                    device_id={axis: me[axis] + step},
                    device_id_type=MESH,
                ).wait_recv()

    arrived(0)

    def put_b(y, plane):
        b[padded(y), :] = plane

    assembled(0, put_b)
    send_faces(0, b, pack_all_z(b))

    arrived(1)

    def put_u(y, plane):
        u[padded(y), :] = plane

    assembled(1, put_u)
    send_faces(1, u, pack_all_z(u))

    migrate(9, 11)
    wait_faces(0)
    b[pl.ds(first - 1, E, stride=ST), :] = hr[0, 0]
    b[pl.ds(first + E, E, stride=ST), :] = hr[0, 1]
    b[pl.ds(8, E), :] = hr[0, 2]
    b[pl.ds(first + E * ST, E), :] = hr[0, 3]
    b_halo = z_halo(0)

    def coefs(y, carry):
        v = b[padded(y), :]
        at = at_plane(y)
        edge = z_edge(b_halo, y)
        x_low = 0.5 * (b[pl.ds(base(y) - 1, E), :] + v)
        x_high = 0.5 * (b[pl.ds(base(y) + 1, E), :] + v)
        y_low = 0.5 * (b[padded(y - 1), :] + v)
        y_high = 0.5 * (b[padded(y + 1), :] + v)
        z_low = 0.5 * (jnp.where(lane == 0, edge, pltpu.roll(v, 1, 1)) + v)
        z_high = 0.5 * (jnp.where(lane == L - 1, edge, pltpu.roll(v, L - 1, 1)) + v)
        cxl[at, :] = x_low
        cxh[at, :] = x_high
        cy[at, :] = y_low
        cy[at_plane(y + 1), :] = y_high
        czl[at, :] = jnp.where(lane == 0, 0.0, z_low)
        czh[at, :] = jnp.where(lane == L - 1, 0.0, z_high)
        ez[at, :] = jnp.where(lane == 0, z_low, jnp.where(lane == L - 1, z_high, 0.0))
        dia[at, :] = (x_high + x_low) + (y_high + y_low) + (z_high + z_low)
        return carry

    lax.fori_loop(0, E, coefs, 0)

    migrate(11, len(steps) + lag)
    arrived(2)

    def put_a(y, plane):
        at = at_plane(y)
        total = plane + dia[at, :]
        inverse = 1.0 / total
        dia[at, :] = total
        inv[at, :] = inverse
        ezi[at, :] = ez[at, :] * inverse

    assembled(2, put_a)
    arrived(3)

    def put_f(y, plane):
        f[at_plane(y), :] = plane

    assembled(3, put_f)

    def neighbours(y):
        at = at_plane(y)
        v = u[padded(y), :]
        x_sum = cxh[at, :] * u[pl.ds(base(y) + 1, E), :] + cxl[at, :] * u[pl.ds(base(y) - 1, E), :]
        y_sum = cy[at_plane(y + 1), :] * u[padded(y + 1), :] + cy[at, :] * u[padded(y - 1), :]
        z_sum = czh[at, :] * pltpu.roll(v, L - 1, 1) + czl[at, :] * pltpu.roll(v, 1, 1)
        return v, x_sum + y_sum + z_sum

    low_x = pl.ds(0, E, stride=E)
    high_x = pl.ds(E - 1, E, stride=E)
    low_y = pl.ds(0, E)
    high_y = pl.ds((E - 1) * E, E)
    top_y = pl.ds(E * E, E)

    e = 1
    for sweep in range(SWEEPS):
        for colour in (0, 1):
            masks = (even, odd) if colour == 0 else (odd, even)

            def planes(t, carry):
                for j in range(4):
                    y = t * 4 + j
                    at = at_plane(y)
                    v, total = neighbours(y)
                    new = (f[at, :] + total) * inv[at, :]
                    u[padded(y), :] = jnp.where(masks[j % 2], new, v)
                return carry

            lax.fori_loop(0, E // 4, planes, 0)
            wait_faces(e)
            for at, mask, term in (
                (pl.ds(first, E, stride=ST), 0, cxl[low_x, :] * inv[low_x, :] * hr[e, 0]),
                (pl.ds(first + E - 1, E, stride=ST), 1, cxh[high_x, :] * inv[high_x, :] * hr[e, 1]),
                (pl.ds(first, E), 0, cy[low_y, :] * inv[low_y, :] * hr[e, 2]),
                (pl.ds(first + (E - 1) * ST, E), 1, cy[top_y, :] * inv[high_y, :] * hr[e, 3]),
            ):
                u[at, :] = u[at, :] + jnp.where(masks[mask], term, 0.0)
            halo = z_halo(e)

            def edges(t, face):
                for j in range(4):
                    y = t * 4 + j
                    term = ezi[at_plane(y), :] * z_edge(halo, y)
                    v = u[padded(y), :] + jnp.where(masks[j % 2], term, 0.0)
                    u[padded(y), :] = v
                    face = pack_z(y, v, face)
                return face

            face = lax.fori_loop(0, E // 4, edges, zero)
            e += 1
            send_faces(e, u, face)

    def residual(t, carry):
        for j in range(4):
            y = t * 4 + j
            at = at_plane(y)
            v, total = neighbours(y)
            res[at, :] = f[at, :] - (dia[at, :] * v - total)
        return carry

    lax.fori_loop(0, E // 4, residual, 0)
    for x in range(E):
        sol_out[x] = u[pl.ds(first + x, E, stride=ST), :]
    wait_faces(e)
    for at, term in (
        (low_x, cxl[low_x, :] * hr[e, 0]),
        (high_x, cxh[high_x, :] * hr[e, 1]),
        (low_y, cy[low_y, :] * hr[e, 2]),
        (high_y, cy[top_y, :] * hr[e, 3]),
    ):
        res[at, :] = res[at, :] + term
    last_halo = z_halo(e)

    def last_edges(t, carry):
        for j in range(4):
            y = t * 4 + j
            at = at_plane(y)
            res[at, :] = res[at, :] + ez[at, :] * z_edge(last_halo, y)
        return carry

    lax.fori_loop(0, E // 4, last_edges, 0)
    for x in range(E):
        res_out[x] = res[pl.ds(x, E, stride=E), :]

    for i, part in steps:
        for way in range(2):

            @pl.when(sends(way))
            def _():
                hop(i, way, part, my_y + 1 - 2 * way).wait_send()

    for exchange in range(e + 1):
        for side in range(6):

            @pl.when(exists(side))
            def _():
                face_copy(exchange, side).wait_send()


def per_device(width, solution_old, right_side, acoef, bcoef, corners):
    n_y = width["gy"]
    exchanges = 2 + 2 * SWEEPS
    box = (E, E * E)
    field = pltpu.VMEM((E * E, L), jnp.float32)
    padded = pltpu.VMEM(((E + 2) * ST + 16, L), jnp.float32)
    faces = pltpu.VMEM((exchanges, 6, E, L), jnp.float32)
    own = pltpu.VMEM((PER,) + box, jnp.float32)
    moved = pltpu.VMEM((2, n_y - 1) + box, jnp.float32)
    half = pltpu.VMEM((2, n_y - 1, E // 2, E * E), jnp.float32)
    out = jax.ShapeDtypeStruct((E, E, L), jnp.float32)
    return pl.pallas_call(
        functools.partial(kernel, width),
        out_shape=(out, out),
        in_specs=[pl.BlockSpec(memory_space=pltpu.SMEM)]
        + [pl.BlockSpec(memory_space=pl.ANY)] * 4,
        out_specs=(pl.BlockSpec(memory_space=pltpu.VMEM),) * 2,
        scratch_shapes=[own] * 4
        + [moved, half, moved, moved] * 2
        + [padded, padded]
        + [field] * 6
        + [pltpu.VMEM(((E + 1) * E, L), jnp.float32)]
        + [field] * 4
        + [faces] * 2
        + [
            pltpu.SemaphoreType.DMA((4,)),
            pltpu.SemaphoreType.DMA((4, 2, 5)),
            pltpu.SemaphoreType.DMA((4, 2, 5)),
            pltpu.SemaphoreType.DMA((exchanges, 6)),
            pltpu.SemaphoreType.DMA((exchanges, 6)),
        ],
        compiler_params=pltpu.CompilerParams(
            collective_id=0, has_side_effects=True, vmem_limit_bytes=64 * 1024 * 1024
        ),
        cost_estimate=pl.CostEstimate(
            flops=100 * E * E * L, bytes_accessed=24 * E * E * L, transcendentals=0
        ),
    )(corners, solution_old, right_side, acoef, bcoef)


def solution(mesh):
    width = dict(mesh.shape)
    boxes = P(("gx", "gy", "gz"), None, None)
    level = P("gx", "gy", "gz")
    return jax.shard_map(
        functools.partial(per_device, width),
        mesh=mesh,
        in_specs=(boxes, boxes, boxes, boxes, P()),
        out_specs=(level, level),
        check_vma=False,
    )
```

```python
import functools

import jax
import jax.numpy as jnp
from jax import lax
from jax.experimental import pallas as pl
from jax.experimental.pallas import tpu as pltpu
from jax.sharding import PartitionSpec as P

SWEEPS = 2
E = 32
L = 128
PER = 4
ST = E + 8
MESH = pl.DeviceIdType.MESH
SIDES = (("gx", -1), ("gx", 1), ("gy", -1), ("gy", 1), ("gz", -1), ("gz", 1))


def kernel(
    width,
    corners,
    sol_in,
    rhs_in,
    abs_in,
    dif_in,
    sol_out,
    res_out,
    own_b,
    own_u,
    own_a,
    own_f,
    st_b,
    st_u,
    st_a,
    st_f,
    rv_b,
    rv_u,
    rv_a,
    rv_f,
    b,
    u,
    f,
    dia,
    inv,
    res,
    cxl,
    cxh,
    cy,
    czl,
    czh,
    ez,
    ezi,
    hs,
    hr,
    in_sem,
    ms_sem,
    mr_sem,
    hs_sem,
    hr_sem,
):
    me = {axis: lax.axis_index(axis) for axis in ("gx", "gy", "gz")}
    n_y = width["gy"]
    my_y = me["gy"]

    loads = [
        pltpu.make_async_copy(src, dst, in_sem.at[i])
        for i, (src, dst) in enumerate(
            ((dif_in, own_b), (sol_in, own_u), (abs_in, own_a), (rhs_in, own_f))
        )
    ]
    for load in loads:
        load.start()

    def exists(side):
        axis, step = SIDES[side]
        return me[axis] > 0 if step < 0 else me[axis] < width[axis] - 1

    hr[...] = jnp.zeros_like(hr)

    barrier = pltpu.get_barrier_semaphore()
    partners = n_y - 1
    for k in range(1, n_y):
        pl.semaphore_signal(
            barrier, inc=1, device_id={"gy": lax.rem(my_y + k, n_y)}, device_id_type=MESH
        )
    for side in (0, 1, 4, 5):
        axis, step = SIDES[side]

        @pl.when(exists(side))
        def _():
            pl.semaphore_signal(
                barrier, inc=1, device_id={axis: me[axis] + step}, device_id_type=MESH
            )

        partners = partners + exists(side).astype(jnp.int32)

    def owner_inner(device, slot):
        row = ((me["gx"] * n_y + device) * width["gz"] + me["gz"]) * PER + slot
        return lax.div(corners[1, row], E), lax.div(lax.rem(corners[2, row], PER * E), E)

    mine = [owner_inner(my_y, s) for s in range(PER)]
    send_slot = []
    for k in range(1, n_y):
        target = lax.rem(my_y + k, n_y)
        slot = jnp.int32(0)
        for s in range(PER):
            slot = jnp.where(mine[s][0] == target, s, slot)
        send_slot.append(slot)
    own_slot = [jnp.int32(0)] * PER
    is_own = [jnp.int32(0)] * PER
    got_slot = [jnp.int32(0)] * PER
    for q in range(PER):
        for s in range(PER):
            here = (mine[s][0] == my_y) & (mine[s][1] == q)
            own_slot[q] = jnp.where(here, s, own_slot[q])
            is_own[q] = jnp.where(here, 1, is_own[q])
    for k in range(1, n_y):
        device = lax.rem(my_y + n_y - k, n_y)
        for s in range(PER):
            owner, inner = owner_inner(device, s)
            for q in range(PER):
                got_slot[q] = jnp.where((owner == my_y) & (inner == q), k - 1, got_slot[q])

    row = lax.broadcasted_iota(jnp.int32, (E, L), 0)
    lane = lax.broadcasted_iota(jnp.int32, (E, L), 1)
    wide_row = lax.broadcasted_iota(jnp.int32, (E // 2, E * E), 0)
    wide_lane = lax.broadcasted_iota(jnp.int32, (E // 2, E * E), 1)
    odd_half = (wide_row + wide_lane // E + wide_lane) % 2 == 1

    def migrate(i, k, st, rv):
        return pltpu.make_async_remote_copy(
            src_ref=st.at[k - 1],
            dst_ref=rv.at[k - 1],
            send_sem=ms_sem.at[i, k - 1],
            recv_sem=mr_sem.at[i, k - 1],
            device_id={"gy": lax.rem(my_y + k, n_y)},
            device_id_type=MESH,
        )

    fields = ((own_b, st_b, rv_b), (own_u, st_u, rv_u), (own_a, st_a, rv_a), (own_f, st_f, rv_f))
    def send_boxes(i):
        own, st, rv = fields[i]
        loads[i].wait()
        for k in range(1, n_y):
            box = own[send_slot[k - 1]]
            if i == 1:
                box = jnp.where(odd_half, box[: E // 2], pltpu.roll(box[E // 2 :], 1, 0))
            st[k - 1] = box
        if i == 0:
            pl.semaphore_wait(barrier, partners)
        for k in range(1, n_y):
            migrate(i, k, st, rv).start()

    for i in range(3):
        send_boxes(i)
    b[...] = jnp.zeros_like(b)
    u[...] = jnp.zeros_like(u)

    def arrived(i):
        _, st, rv = fields[i]
        for k in range(1, n_y):
            migrate(i, k, st, rv).wait_recv()

    group = lane // E
    own_mask = [jnp.full((E, L), is_own[q], jnp.int32) == 1 for q in range(PER)]

    def assembled(i, put, carry=0):
        own, _, rv = fields[i]

        def columns(t, carry):
            at = pl.ds(pl.multiple_of(t * L, L), L)
            parts = []
            for q in range(PER):
                got = rv[got_slot[q], :, at]
                if i == 1:
                    got = jnp.concatenate([got, pltpu.roll(got, E // 2 - 1, 0)], axis=0)
                parts.append(jnp.where(own_mask[q], own[own_slot[q], :, at], got))
            for j in range(PER):
                plane = parts[j]
                for q in range(PER):
                    if q != j:
                        plane = jnp.where(
                            group == q, pltpu.roll(parts[q], (q - j) * E % L, 1), plane
                        )
                carry = put(t * PER + j, j, plane, carry)
            return carry

        return lax.fori_loop(0, E * E // L, columns, carry)

    def at_plane(y):
        return pl.ds(pl.multiple_of(y * E, E), E)

    def base(y):
        return pl.multiple_of(y * ST + ST + 8, 8)

    def padded(y):
        return pl.ds(base(y), E)

    even = (row + lane) % 2 == 0
    odd = (row + lane) % 2 == 1
    pair = lane // 2
    zero = jnp.zeros((E, L), jnp.float32)
    first = ST + 8

    def pack_z(y, v, face):
        return jnp.where(pair == y, pltpu.roll(v, 2 * y + 1, 1), face)

    def pack_all_z(ref):
        def planes(t, face):
            for j in range(4):
                y = t * 4 + j
                face = pack_z(y, ref[padded(y), :], face)
            return face

        return lax.fori_loop(0, E // 4, planes, zero)

    def z_halo(e):
        return jnp.where(lane % 2 == 0, hr[e, 4], pltpu.roll(hr[e, 5], L - 2, 1))

    def z_edge(halo, y):
        return pltpu.roll(halo, lax.rem(L - 2 * y, L), 1)

    def face_copy(e, side):
        axis, step = SIDES[side]
        return pltpu.make_async_remote_copy(
            src_ref=hs.at[e, side],
            dst_ref=hr.at[e, side ^ 1],
            send_sem=hs_sem.at[e, side],
            recv_sem=hr_sem.at[e, side ^ 1],
            device_id={axis: me[axis] + step},
            device_id_type=MESH,
        )

    def send_faces(e, ref, z_face):
        hs[e, 0] = ref[pl.ds(first, E, stride=ST), :]
        hs[e, 1] = ref[pl.ds(first + E - 1, E, stride=ST), :]
        hs[e, 2] = ref[pl.ds(first, E), :]
        hs[e, 3] = ref[pl.ds(first + (E - 1) * ST, E), :]
        hs[e, 4] = z_face
        hs[e, 5] = z_face
        for side in range(6):

            @pl.when(exists(side))
            def _():
                face_copy(e, side).start()

    def wait_faces(e):
        for side in range(6):
            axis, step = SIDES[side]

            @pl.when(exists(side))
            def _():
                pltpu.make_async_remote_copy(
                    src_ref=hs.at[e, side],
                    dst_ref=hr.at[e, side],
                    send_sem=hs_sem.at[e, side],
                    recv_sem=hr_sem.at[e, side],
                    device_id={axis: me[axis] + step},
                    device_id_type=MESH,
                ).wait_recv()

    arrived(0)

    def put_b(y, j, plane, carry):
        b[padded(y), :] = plane
        return carry

    assembled(0, put_b)
    send_faces(0, b, pack_all_z(b))

    arrived(1)

    def put_u(y, j, plane, carry):
        u[padded(y), :] = plane
        return carry

    assembled(1, put_u)
    send_faces(1, u, pack_all_z(u))
    send_boxes(3)

    wait_faces(0)
    b[pl.ds(first - 1, E, stride=ST), :] = hr[0, 0]
    b[pl.ds(first + E, E, stride=ST), :] = hr[0, 1]
    b[pl.ds(8, E), :] = hr[0, 2]
    b[pl.ds(first + E * ST, E), :] = hr[0, 3]
    b_halo = z_halo(0)

    def coefs(y, carry):
        v = b[padded(y), :]
        at = at_plane(y)
        edge = z_edge(b_halo, y)
        x_low = 0.5 * (b[pl.ds(base(y) - 1, E), :] + v)
        x_high = 0.5 * (b[pl.ds(base(y) + 1, E), :] + v)
        y_low = 0.5 * (b[padded(y - 1), :] + v)
        y_high = 0.5 * (b[padded(y + 1), :] + v)
        z_low = 0.5 * (jnp.where(lane == 0, edge, pltpu.roll(v, 1, 1)) + v)
        z_high = 0.5 * (jnp.where(lane == L - 1, edge, pltpu.roll(v, L - 1, 1)) + v)
        cxl[at, :] = x_low
        cxh[at, :] = x_high
        cy[at, :] = y_low
        cy[at_plane(y + 1), :] = y_high
        czl[at, :] = jnp.where(lane == 0, 0.0, z_low)
        czh[at, :] = jnp.where(lane == L - 1, 0.0, z_high)
        ez[at, :] = jnp.where(lane == 0, z_low, jnp.where(lane == L - 1, z_high, 0.0))
        dia[at, :] = (x_high + x_low) + (y_high + y_low) + (z_high + z_low)
        return carry

    lax.fori_loop(0, E, coefs, 0)

    arrived(2)

    def put_a(y, j, plane, carry):
        at = at_plane(y)
        total = plane + dia[at, :]
        inverse = 1.0 / total
        dia[at, :] = total
        inv[at, :] = inverse
        ezi[at, :] = ez[at, :] * inverse
        return carry

    assembled(2, put_a)

    def neighbours(y):
        at = at_plane(y)
        v = u[padded(y), :]
        x_sum = cxh[at, :] * u[pl.ds(base(y) + 1, E), :] + cxl[at, :] * u[pl.ds(base(y) - 1, E), :]
        y_sum = cy[at_plane(y + 1), :] * u[padded(y + 1), :] + cy[at, :] * u[padded(y - 1), :]
        z_sum = czh[at, :] * pltpu.roll(v, L - 1, 1) + czl[at, :] * pltpu.roll(v, 1, 1)
        return v, x_sum + y_sum + z_sum

    low_x = pl.ds(0, E, stride=E)
    high_x = pl.ds(E - 1, E, stride=E)
    low_y = pl.ds(0, E)
    high_y = pl.ds((E - 1) * E, E)
    top_y = pl.ds(E * E, E)

    def add_faces(e):
        for at, term in (
            (low_x, cxl[low_x, :] * hr[e, 0]),
            (high_x, cxh[high_x, :] * hr[e, 1]),
            (low_y, cy[low_y, :] * hr[e, 2]),
            (high_y, cy[top_y, :] * hr[e, 3]),
        ):
            res[at, :] = res[at, :] + term

    wait_faces(1)
    first_halo = z_halo(1)

    def first_sums(t, carry):
        for j in range(4):
            y = t * 4 + j
            at = at_plane(y)
            res[at, :] = neighbours(y)[1] + ez[at, :] * z_edge(first_halo, y)
        return carry

    lax.fori_loop(0, E // 4, first_sums, 0)
    add_faces(1)
    arrived(3)

    def put_f(y, j, plane, face):
        at = at_plane(y)
        f[at, :] = plane
        new = (plane + res[at, :]) * inv[at, :]
        v = jnp.where(even if j % 2 == 0 else odd, new, u[padded(y), :])
        u[padded(y), :] = v
        return pack_z(y, v, face)

    send_faces(2, u, assembled(3, put_f, zero))

    e = 2
    for sweep in range(SWEEPS):
        for colour in (0, 1):
            if sweep == 0 and colour == 0:
                continue
            masks = (even, odd) if colour == 0 else (odd, even)

            def planes(t, carry):
                for j in range(4):
                    y = t * 4 + j
                    at = at_plane(y)
                    v, total = neighbours(y)
                    new = (f[at, :] + total) * inv[at, :]
                    u[padded(y), :] = jnp.where(masks[j % 2], new, v)
                return carry

            lax.fori_loop(0, E // 4, planes, 0)
            wait_faces(e)
            for at, mask, term in (
                (pl.ds(first, E, stride=ST), 0, cxl[low_x, :] * inv[low_x, :] * hr[e, 0]),
                (pl.ds(first + E - 1, E, stride=ST), 1, cxh[high_x, :] * inv[high_x, :] * hr[e, 1]),
                (pl.ds(first, E), 0, cy[low_y, :] * inv[low_y, :] * hr[e, 2]),
                (pl.ds(first + (E - 1) * ST, E), 1, cy[top_y, :] * inv[high_y, :] * hr[e, 3]),
            ):
                u[at, :] = u[at, :] + jnp.where(masks[mask], term, 0.0)
            halo = z_halo(e)

            def edges(t, face):
                for j in range(4):
                    y = t * 4 + j
                    term = ezi[at_plane(y), :] * z_edge(halo, y)
                    v = u[padded(y), :] + jnp.where(masks[j % 2], term, 0.0)
                    u[padded(y), :] = v
                    face = pack_z(y, v, face)
                return face

            face = lax.fori_loop(0, E // 4, edges, zero)
            e += 1
            send_faces(e, u, face)

    def residual(t, carry):
        for j in range(4):
            y = t * 4 + j
            at = at_plane(y)
            v, total = neighbours(y)
            res[at, :] = f[at, :] - (dia[at, :] * v - total)
        return carry

    lax.fori_loop(0, E // 4, residual, 0)
    for x in range(E):
        sol_out[x] = u[pl.ds(first + x, E, stride=ST), :]
    wait_faces(e)
    add_faces(e)
    last_halo = z_halo(e)

    def last_edges(t, carry):
        for j in range(4):
            y = t * 4 + j
            at = at_plane(y)
            res[at, :] = res[at, :] + ez[at, :] * z_edge(last_halo, y)
        return carry

    lax.fori_loop(0, E // 4, last_edges, 0)
    for x in range(E):
        res_out[x] = res[pl.ds(x, E, stride=E), :]

    for i, (_, st, rv) in enumerate(fields):
        for k in range(1, n_y):
            migrate(i, k, st, rv).wait_send()
    for exchange in range(e + 1):
        for side in range(6):

            @pl.when(exists(side))
            def _():
                face_copy(exchange, side).wait_send()


def per_device(width, solution_old, right_side, acoef, bcoef, corners):
    n_y = width["gy"]
    exchanges = 2 + 2 * SWEEPS
    box = (E, E * E)
    field = pltpu.VMEM((E * E, L), jnp.float32)
    padded = pltpu.VMEM(((E + 2) * ST + 16, L), jnp.float32)
    faces = pltpu.VMEM((exchanges, 6, E, L), jnp.float32)
    own = pltpu.VMEM((PER,) + box, jnp.float32)
    moved = pltpu.VMEM((n_y - 1,) + box, jnp.float32)
    half = pltpu.VMEM((n_y - 1, E // 2, E * E), jnp.float32)
    out = jax.ShapeDtypeStruct((E, E, L), jnp.float32)
    return pl.pallas_call(
        functools.partial(kernel, width),
        out_shape=(out, out),
        in_specs=[pl.BlockSpec(memory_space=pltpu.SMEM)]
        + [pl.BlockSpec(memory_space=pl.ANY)] * 4,
        out_specs=(pl.BlockSpec(memory_space=pltpu.VMEM),) * 2,
        scratch_shapes=[own] * 4
        + [moved, half, moved, moved] * 2
        + [padded, padded]
        + [field] * 6
        + [pltpu.VMEM(((E + 1) * E, L), jnp.float32)]
        + [field] * 4
        + [faces] * 2
        + [
            pltpu.SemaphoreType.DMA((4,)),
            pltpu.SemaphoreType.DMA((4, n_y - 1)),
            pltpu.SemaphoreType.DMA((4, n_y - 1)),
            pltpu.SemaphoreType.DMA((exchanges, 6)),
            pltpu.SemaphoreType.DMA((exchanges, 6)),
        ],
        compiler_params=pltpu.CompilerParams(
            collective_id=0, has_side_effects=True, vmem_limit_bytes=64 * 1024 * 1024
        ),
        cost_estimate=pl.CostEstimate(
            flops=100 * E * E * L, bytes_accessed=24 * E * E * L, transcendentals=0
        ),
    )(corners, solution_old, right_side, acoef, bcoef)


def solution(mesh):
    width = dict(mesh.shape)
    boxes = P(("gx", "gy", "gz"), None, None)
    level = P("gx", "gy", "gz")
    return jax.shard_map(
        functools.partial(per_device, width),
        mesh=mesh,
        in_specs=(boxes, boxes, boxes, boxes, P()),
        out_specs=(level, level),
        check_vma=False,
    )
```

```python
import functools

import jax
import jax.numpy as jnp
from jax import lax
from jax.experimental import pallas as pl
from jax.experimental.pallas import tpu as pltpu
from jax.sharding import PartitionSpec as P

SWEEPS = 2
E = 32
L = 128
PER = 4
ST = E + 8
MESH = pl.DeviceIdType.MESH
SIDES = (("gx", -1), ("gx", 1), ("gy", -1), ("gy", 1), ("gz", -1), ("gz", 1))


def kernel(
    width,
    corners,
    sol_in,
    rhs_in,
    abs_in,
    dif_in,
    sol_out,
    res_out,
    own_b,
    own_u,
    own_a,
    own_f,
    st_b,
    st_u,
    st_a,
    st_f,
    rv_b,
    rv_u,
    rv_a,
    rv_f,
    b,
    u,
    f,
    dia,
    inv,
    res,
    cxl,
    cxh,
    cy,
    czl,
    czh,
    ez,
    ezi,
    hs,
    hr,
    in_sem,
    ms_sem,
    mr_sem,
    hs_sem,
    hr_sem,
):
    me = {axis: lax.axis_index(axis) for axis in ("gx", "gy", "gz")}
    n_y = width["gy"]
    my_y = me["gy"]

    loads = [
        pltpu.make_async_copy(src, dst, in_sem.at[i])
        for i, (src, dst) in enumerate(
            ((dif_in, own_b), (sol_in, own_u), (abs_in, own_a), (rhs_in, own_f))
        )
    ]
    for load in loads:
        load.start()

    def exists(side):
        axis, step = SIDES[side]
        return me[axis] > 0 if step < 0 else me[axis] < width[axis] - 1

    hr[...] = jnp.zeros_like(hr)

    barrier = pltpu.get_barrier_semaphore()
    partners = 0
    for side in range(6):
        axis, step = SIDES[side]

        @pl.when(exists(side))
        def _():
            pl.semaphore_signal(
                barrier, inc=1, device_id={axis: me[axis] + step}, device_id_type=MESH
            )

        partners = partners + exists(side).astype(jnp.int32)

    def owner_inner(device, slot):
        row = ((me["gx"] * n_y + device) * width["gz"] + me["gz"]) * PER + slot
        return lax.div(corners[1, row], E), lax.div(lax.rem(corners[2, row], PER * E), E)

    table = [[owner_inner(j, s) for s in range(PER)] for j in range(n_y)]
    goes, its_slot, its_inner = {}, {}, {}
    for j in range(n_y):
        for t in range(n_y):
            if t != j:
                live, slot, inner = jnp.int32(0), jnp.int32(0), jnp.int32(0)
                for s in range(PER):
                    hit = table[j][s][0] == t
                    live = jnp.where(hit, 1, live)
                    slot = jnp.where(hit, s, slot)
                    inner = jnp.where(hit, table[j][s][1], inner)
                goes[j, t], its_slot[j, t], its_inner[j, t] = live, slot, inner

    n_slot = n_y - 1
    rank = {}
    code = [[jnp.int32(0)] * n_slot for _ in range(2)]
    for way in range(2):
        for c in range(n_y):
            at = (lambda i: i) if way == 0 else (lambda i: n_y - 1 - i)
            here = [jnp.int32(0)] * n_slot
            count = jnp.int32(0)
            for t in range(n_y - 1, c, -1):
                for j in range(c + 1):
                    pair = (at(j), at(t))
                    rank[way, c, j, t] = count
                    held = its_slot[pair] if j == c else PER + rank[way, c - 1, j, t]
                    for k in range(n_slot):
                        here[k] = jnp.where((goes[pair] == 1) & (count == k), held, here[k])
                    count = count + goes[pair]
            for k in range(n_slot):
                code[way][k] = jnp.where(my_y == at(c), here[k], code[way][k])

    inward = jnp.where(my_y < n_y // 2, 0, 1)
    outward = 1 - inward

    row = lax.broadcasted_iota(jnp.int32, (E, L), 0)
    lane = lax.broadcasted_iota(jnp.int32, (E, L), 1)
    wide_row = lax.broadcasted_iota(jnp.int32, (E // 2, E * E), 0)
    wide_lane = lax.broadcasted_iota(jnp.int32, (E // 2, E * E), 1)
    odd_half = (wide_row + wide_lane // E + wide_lane) % 2 == 1

    fields = ((own_b, st_b, rv_b), (own_u, st_u, rv_u), (own_a, st_a, rv_a), (own_f, st_f, rv_f))
    chunks = (4, 1, 2, 2)

    def part_of(ref, i, way, part):
        if part == chunks[i]:
            return ref.at[way, n_slot - 1]
        rows = ref.shape[2] // chunks[i]
        return ref.at[way, pl.ds(0, n_slot - 1), pl.ds(part * rows, rows)]

    def hop(i, way, part, neighbour):
        _, st, rv = fields[i]
        return pltpu.make_async_remote_copy(
            src_ref=part_of(st, i, way, part),
            dst_ref=part_of(rv, i, way, part),
            send_sem=ms_sem.at[i, way, part],
            recv_sem=mr_sem.at[i, way, part],
            device_id={"gy": neighbour},
            device_id_type=MESH,
        )

    def sends(way):
        return jnp.where(way == 0, my_y < n_y - 1, my_y > 0)

    def receives(way):
        return jnp.where(way == 0, my_y > 0, my_y < n_y - 1)

    def fill(i, way, k, start, rows, relays=True):
        own, st, rv = fields[i]
        held = jnp.where(way == 0, code[0][k], code[1][k])
        slot = jnp.where(held < PER, held, 0)
        if i == 1:
            box = own[slot]
            box = jnp.where(odd_half, box[: E // 2], pltpu.roll(box[E // 2 :], 1, 0))
        else:
            box = own[slot, pl.ds(start, rows), :]
        for r in range(n_slot - 1 if relays else 0):
            relayed = jnp.full((rows, E * E), held, jnp.int32) == PER + r
            box = jnp.where(relayed, rv[way, r, pl.ds(start, rows), :], box)
        st[way, k, pl.ds(start, rows), :] = box

    def take_hop(i, way, part):
        @pl.when(receives(way))
        def _():
            hop(i, way, part, my_y - 1 + 2 * way).wait_recv()

    def pass_on(i, way, part, relays=True):
        @pl.when(sends(way))
        def _():
            rows = fields[i][1].shape[2]
            if part < chunks[i]:
                take_hop(i, way, part)
                rows = rows // chunks[i]
                for k in range(n_slot - 1):
                    fill(i, way, k, part * rows, rows)
            else:
                fill(i, way, n_slot - 1, 0, rows, relays)
            hop(i, way, part, my_y + 1 - 2 * way).start()

    steps = [(i, part) for i in range(4) for part in range(chunks[i] + 1)]
    lag = 2
    ahead = n_y <= 4

    def end_sends(i, parts):
        @pl.when(jnp.logical_not(receives(inward)))
        def _():
            for part in parts:
                pass_on(i, inward, part, relays=False)

    def last_out(i):
        if ahead:
            pass_on(i, outward, chunks[i], relays=False)

    def middle(first_step, last_step):
        @pl.when(receives(inward))
        def _():
            for n in range(first_step, last_step):
                if n < len(steps):
                    pass_on(steps[n][0], inward, steps[n][1])
                if 0 <= n - lag < len(steps):
                    i, part = steps[n - lag]
                    if not (ahead and part == chunks[i]):
                        pass_on(i, outward, part)

    def arrived(i):
        for way in range(2):

            @pl.when(jnp.logical_not(sends(way)))
            def _():
                for part in range(chunks[i]):
                    take_hop(i, way, part)

            take_hop(i, way, chunks[i])

    for i in range(3):
        loads[i].wait()
        if i == 0:
            pl.semaphore_wait(barrier, partners)
        end_sends(i, range(chunks[i] + 1))
    last_out(0)
    last_out(1)
    middle(0, 7)
    last_out(2)
    middle(7, 9)
    b[...] = jnp.zeros_like(b)
    u[...] = jnp.zeros_like(u)

    own_slot = [jnp.int32(0)] * PER
    is_own = [jnp.int32(0)] * PER
    got_slot = [jnp.int32(0)] * PER
    got_way = [jnp.int32(0)] * PER
    for q in range(PER):
        for s in range(PER):
            owner, inner = owner_inner(my_y, s)
            here = (owner == my_y) & (inner == q)
            own_slot[q] = jnp.where(here, s, own_slot[q])
            is_own[q] = jnp.where(here, 1, is_own[q])
        for way in range(2):
            for t in range(1, n_y):
                for j in range(t):
                    pair = (j, t) if way == 0 else (n_y - 1 - j, n_y - 1 - t)
                    here = (goes[pair] == 1) & (its_inner[pair] == q) & (my_y == pair[1])
                    slot = jnp.minimum(rank[way, t - 1, j, t], n_slot - 1)
                    got_slot[q] = jnp.where(here, slot, got_slot[q])
                    got_way[q] = jnp.where(here, way, got_way[q])

    group = lane // E
    own_mask = [jnp.full((E, L), is_own[q], jnp.int32) == 1 for q in range(PER)]

    def assembled(i, put, carry=0):
        own, _, rv = fields[i]

        def columns(t, carry):
            at = pl.ds(pl.multiple_of(t * L, L), L)
            parts = []
            for q in range(PER):
                got = rv[got_way[q], got_slot[q], :, at]
                if i == 1:
                    got = jnp.concatenate([got, pltpu.roll(got, E // 2 - 1, 0)], axis=0)
                parts.append(jnp.where(own_mask[q], own[own_slot[q], :, at], got))
            for j in range(PER):
                plane = parts[j]
                for q in range(PER):
                    if q != j:
                        plane = jnp.where(
                            group == q, pltpu.roll(parts[q], (q - j) * E % L, 1), plane
                        )
                carry = put(t * PER + j, j, plane, carry)
            return carry

        return lax.fori_loop(0, E * E // L, columns, carry)

    def at_plane(y):
        return pl.ds(pl.multiple_of(y * E, E), E)

    def base(y):
        return pl.multiple_of(y * ST + ST + 8, 8)

    def padded(y):
        return pl.ds(base(y), E)

    even = (row + lane) % 2 == 0
    odd = (row + lane) % 2 == 1
    pair = lane // 2
    zero = jnp.zeros((E, L), jnp.float32)
    first = ST + 8

    def pack_z(y, v, face):
        return jnp.where(pair == y, pltpu.roll(v, 2 * y + 1, 1), face)

    def pack_all_z(ref):
        def planes(t, face):
            for j in range(4):
                y = t * 4 + j
                face = pack_z(y, ref[padded(y), :], face)
            return face

        return lax.fori_loop(0, E // 4, planes, zero)

    def z_halo(e):
        return jnp.where(lane % 2 == 0, hr[e, 4], pltpu.roll(hr[e, 5], L - 2, 1))

    def z_edge(halo, y):
        return pltpu.roll(halo, lax.rem(L - 2 * y, L), 1)

    def face_copy(e, side):
        axis, step = SIDES[side]
        return pltpu.make_async_remote_copy(
            src_ref=hs.at[e, side],
            dst_ref=hr.at[e, side ^ 1],
            send_sem=hs_sem.at[e, side],
            recv_sem=hr_sem.at[e, side ^ 1],
            device_id={axis: me[axis] + step},
            device_id_type=MESH,
        )

    def send_faces(e, ref, z_face):
        hs[e, 0] = ref[pl.ds(first, E, stride=ST), :]
        hs[e, 1] = ref[pl.ds(first + E - 1, E, stride=ST), :]
        hs[e, 2] = ref[pl.ds(first, E), :]
        hs[e, 3] = ref[pl.ds(first + (E - 1) * ST, E), :]
        hs[e, 4] = z_face
        hs[e, 5] = z_face
        for side in range(6):

            @pl.when(exists(side))
            def _():
                face_copy(e, side).start()

    def wait_faces(e):
        for side in range(6):
            axis, step = SIDES[side]

            @pl.when(exists(side))
            def _():
                pltpu.make_async_remote_copy(
                    src_ref=hs.at[e, side],
                    dst_ref=hr.at[e, side],
                    send_sem=hs_sem.at[e, side],
                    recv_sem=hr_sem.at[e, side],
                    device_id={axis: me[axis] + step},
                    device_id_type=MESH,
                ).wait_recv()

    arrived(0)

    def put_b(y, j, plane, carry):
        b[padded(y), :] = plane
        return carry

    assembled(0, put_b)
    send_faces(0, b, pack_all_z(b))

    loads[3].wait()
    end_sends(3, (0,))
    middle(9, 10)

    arrived(1)

    def put_u(y, j, plane, carry):
        u[padded(y), :] = plane
        return carry

    assembled(1, put_u)
    send_faces(1, u, pack_all_z(u))

    end_sends(3, (1, 2))
    last_out(3)
    middle(10, 11)

    wait_faces(0)
    b[pl.ds(first - 1, E, stride=ST), :] = hr[0, 0]
    b[pl.ds(first + E, E, stride=ST), :] = hr[0, 1]
    b[pl.ds(8, E), :] = hr[0, 2]
    b[pl.ds(first + E * ST, E), :] = hr[0, 3]
    b_halo = z_halo(0)

    def coefs(y, carry):
        v = b[padded(y), :]
        at = at_plane(y)
        edge = z_edge(b_halo, y)
        x_low = 0.5 * (b[pl.ds(base(y) - 1, E), :] + v)
        x_high = 0.5 * (b[pl.ds(base(y) + 1, E), :] + v)
        y_low = 0.5 * (b[padded(y - 1), :] + v)
        y_high = 0.5 * (b[padded(y + 1), :] + v)
        z_low = 0.5 * (jnp.where(lane == 0, edge, pltpu.roll(v, 1, 1)) + v)
        z_high = 0.5 * (jnp.where(lane == L - 1, edge, pltpu.roll(v, L - 1, 1)) + v)
        cxl[at, :] = x_low
        cxh[at, :] = x_high
        cy[at, :] = y_low
        cy[at_plane(y + 1), :] = y_high
        czl[at, :] = jnp.where(lane == 0, 0.0, z_low)
        czh[at, :] = jnp.where(lane == L - 1, 0.0, z_high)
        ez[at, :] = jnp.where(lane == 0, z_low, jnp.where(lane == L - 1, z_high, 0.0))
        dia[at, :] = (x_high + x_low) + (y_high + y_low) + (z_high + z_low)
        return carry

    lax.fori_loop(0, E, coefs, 0)

    middle(11, 12)
    arrived(2)

    def put_a(y, j, plane, carry):
        at = at_plane(y)
        total = plane + dia[at, :]
        inverse = 1.0 / total
        dia[at, :] = total
        inv[at, :] = inverse
        ezi[at, :] = ez[at, :] * inverse
        return carry

    assembled(2, put_a)

    def neighbours(y):
        at = at_plane(y)
        v = u[padded(y), :]
        x_sum = cxh[at, :] * u[pl.ds(base(y) + 1, E), :] + cxl[at, :] * u[pl.ds(base(y) - 1, E), :]
        y_sum = cy[at_plane(y + 1), :] * u[padded(y + 1), :] + cy[at, :] * u[padded(y - 1), :]
        z_sum = czh[at, :] * pltpu.roll(v, L - 1, 1) + czl[at, :] * pltpu.roll(v, 1, 1)
        return v, x_sum + y_sum + z_sum

    low_x = pl.ds(0, E, stride=E)
    high_x = pl.ds(E - 1, E, stride=E)
    low_y = pl.ds(0, E)
    high_y = pl.ds((E - 1) * E, E)
    top_y = pl.ds(E * E, E)

    def add_faces(e):
        for at, term in (
            (low_x, cxl[low_x, :] * hr[e, 0]),
            (high_x, cxh[high_x, :] * hr[e, 1]),
            (low_y, cy[low_y, :] * hr[e, 2]),
            (high_y, cy[top_y, :] * hr[e, 3]),
        ):
            res[at, :] = res[at, :] + term

    middle(12, len(steps) + lag)
    wait_faces(1)
    first_halo = z_halo(1)

    def first_sums(t, carry):
        for j in range(4):
            y = t * 4 + j
            at = at_plane(y)
            res[at, :] = neighbours(y)[1] + ez[at, :] * z_edge(first_halo, y)
        return carry

    lax.fori_loop(0, E // 4, first_sums, 0)
    add_faces(1)
    arrived(3)

    def put_f(y, j, plane, face):
        at = at_plane(y)
        f[at, :] = plane
        new = (plane + res[at, :]) * inv[at, :]
        v = jnp.where(even if j % 2 == 0 else odd, new, u[padded(y), :])
        u[padded(y), :] = v
        return pack_z(y, v, face)

    send_faces(2, u, assembled(3, put_f, zero))

    e = 2
    for sweep in range(SWEEPS):
        for colour in (0, 1):
            if sweep == 0 and colour == 0:
                continue
            masks = (even, odd) if colour == 0 else (odd, even)

            def planes(t, carry):
                for j in range(4):
                    y = t * 4 + j
                    at = at_plane(y)
                    v, total = neighbours(y)
                    new = (f[at, :] + total) * inv[at, :]
                    u[padded(y), :] = jnp.where(masks[j % 2], new, v)
                return carry

            lax.fori_loop(0, E // 4, planes, 0)
            wait_faces(e)
            for at, mask, term in (
                (pl.ds(first, E, stride=ST), 0, cxl[low_x, :] * inv[low_x, :] * hr[e, 0]),
                (pl.ds(first + E - 1, E, stride=ST), 1, cxh[high_x, :] * inv[high_x, :] * hr[e, 1]),
                (pl.ds(first, E), 0, cy[low_y, :] * inv[low_y, :] * hr[e, 2]),
                (pl.ds(first + (E - 1) * ST, E), 1, cy[top_y, :] * inv[high_y, :] * hr[e, 3]),
            ):
                u[at, :] = u[at, :] + jnp.where(masks[mask], term, 0.0)
            halo = z_halo(e)

            def edges(t, face):
                for j in range(4):
                    y = t * 4 + j
                    term = ezi[at_plane(y), :] * z_edge(halo, y)
                    v = u[padded(y), :] + jnp.where(masks[j % 2], term, 0.0)
                    u[padded(y), :] = v
                    face = pack_z(y, v, face)
                return face

            face = lax.fori_loop(0, E // 4, edges, zero)
            e += 1
            send_faces(e, u, face)

    def residual(t, carry):
        for j in range(4):
            y = t * 4 + j
            at = at_plane(y)
            v, total = neighbours(y)
            res[at, :] = f[at, :] - (dia[at, :] * v - total)
        return carry

    lax.fori_loop(0, E // 4, residual, 0)
    for x in range(E):
        sol_out[x] = u[pl.ds(first + x, E, stride=ST), :]
    wait_faces(e)
    add_faces(e)
    last_halo = z_halo(e)

    def last_edges(t, carry):
        for j in range(4):
            y = t * 4 + j
            at = at_plane(y)
            res[at, :] = res[at, :] + ez[at, :] * z_edge(last_halo, y)
        return carry

    lax.fori_loop(0, E // 4, last_edges, 0)
    for x in range(E):
        res_out[x] = res[pl.ds(x, E, stride=E), :]

    for i, part in steps:
        for way in range(2):

            @pl.when(sends(way))
            def _():
                hop(i, way, part, my_y + 1 - 2 * way).wait_send()

    for exchange in range(e + 1):
        for side in range(6):

            @pl.when(exists(side))
            def _():
                face_copy(exchange, side).wait_send()


def per_device(width, solution_old, right_side, acoef, bcoef, corners):
    n_y = width["gy"]
    exchanges = 2 + 2 * SWEEPS
    box = (E, E * E)
    field = pltpu.VMEM((E * E, L), jnp.float32)
    padded = pltpu.VMEM(((E + 2) * ST + 16, L), jnp.float32)
    faces = pltpu.VMEM((exchanges, 6, E, L), jnp.float32)
    own = pltpu.VMEM((PER,) + box, jnp.float32)
    moved = pltpu.VMEM((2, n_y - 1) + box, jnp.float32)
    half = pltpu.VMEM((2, n_y - 1, E // 2, E * E), jnp.float32)
    out = jax.ShapeDtypeStruct((E, E, L), jnp.float32)
    return pl.pallas_call(
        functools.partial(kernel, width),
        out_shape=(out, out),
        in_specs=[pl.BlockSpec(memory_space=pltpu.SMEM)]
        + [pl.BlockSpec(memory_space=pl.ANY)] * 4,
        out_specs=(pl.BlockSpec(memory_space=pltpu.VMEM),) * 2,
        scratch_shapes=[own] * 4
        + [moved, half, moved, moved] * 2
        + [padded, padded]
        + [field] * 6
        + [pltpu.VMEM(((E + 1) * E, L), jnp.float32)]
        + [field] * 4
        + [faces] * 2
        + [
            pltpu.SemaphoreType.DMA((4,)),
            pltpu.SemaphoreType.DMA((4, 2, 5)),
            pltpu.SemaphoreType.DMA((4, 2, 5)),
            pltpu.SemaphoreType.DMA((exchanges, 6)),
            pltpu.SemaphoreType.DMA((exchanges, 6)),
        ],
        compiler_params=pltpu.CompilerParams(
            collective_id=0, has_side_effects=True, vmem_limit_bytes=64 * 1024 * 1024
        ),
        cost_estimate=pl.CostEstimate(
            flops=100 * E * E * L, bytes_accessed=24 * E * E * L, transcendentals=0
        ),
    )(corners, solution_old, right_side, acoef, bcoef)


def solution(mesh):
    width = dict(mesh.shape)
    boxes = P(("gx", "gy", "gz"), None, None)
    level = P("gx", "gy", "gz")
    return jax.shard_map(
        functools.partial(per_device, width),
        mesh=mesh,
        in_specs=(boxes, boxes, boxes, boxes, P()),
        out_specs=(level, level),
        check_vma=False,
    )
```

```python
import functools

import jax
import jax.numpy as jnp
from jax import lax
from jax.experimental import pallas as pl
from jax.experimental.pallas import tpu as pltpu
from jax.sharding import PartitionSpec as P

SWEEPS = 2
E = 32
L = 128
PER = 4
ST = E + 8
MESH = pl.DeviceIdType.MESH
SIDES = (("gx", -1), ("gx", 1), ("gy", -1), ("gy", 1), ("gz", -1), ("gz", 1))


def kernel(
    width,
    corners,
    sol_in,
    rhs_in,
    abs_in,
    dif_in,
    sol_out,
    res_out,
    own_b,
    own_u,
    own_a,
    own_f,
    st_b,
    st_u,
    st_a,
    st_f,
    rv_b,
    rv_u,
    rv_a,
    rv_f,
    b,
    u,
    f,
    dia,
    inv,
    res,
    cxl,
    cxh,
    cy,
    czl,
    czh,
    ez,
    ezi,
    hs,
    hr,
    in_sem,
    ms_sem,
    mr_sem,
    hs_sem,
    hr_sem,
):
    me = {axis: lax.axis_index(axis) for axis in ("gx", "gy", "gz")}
    n_y = width["gy"]
    my_y = me["gy"]

    loads = [
        [
            pltpu.make_async_copy(src.at[q], dst.at[q], in_sem.at[i, q])
            for q in range(PER)
        ]
        for i, (src, dst) in enumerate(
            ((dif_in, own_b), (sol_in, own_u), (abs_in, own_a), (rhs_in, own_f))
        )
    ]
    for field_loads in loads:
        for load in field_loads:
            load.start()

    def loaded(i):
        for load in loads[i]:
            load.wait()

    def exists(side):
        axis, step = SIDES[side]
        return me[axis] > 0 if step < 0 else me[axis] < width[axis] - 1

    hr[...] = jnp.zeros_like(hr)

    barrier = pltpu.get_barrier_semaphore()
    partners = 0
    for side in range(6):
        axis, step = SIDES[side]

        @pl.when(exists(side))
        def _():
            pl.semaphore_signal(
                barrier, inc=1, device_id={axis: me[axis] + step}, device_id_type=MESH
            )

        partners = partners + exists(side).astype(jnp.int32)

    def owner_inner(device, slot):
        row = ((me["gx"] * n_y + device) * width["gz"] + me["gz"]) * PER + slot
        return lax.div(corners[1, row], E), lax.div(lax.rem(corners[2, row], PER * E), E)

    table = [[owner_inner(j, s) for s in range(PER)] for j in range(n_y)]
    goes, its_slot, its_inner = {}, {}, {}
    for j in range(n_y):
        for t in range(n_y):
            if t != j:
                live, slot, inner = jnp.int32(0), jnp.int32(0), jnp.int32(0)
                for s in range(PER):
                    hit = table[j][s][0] == t
                    live = jnp.where(hit, 1, live)
                    slot = jnp.where(hit, s, slot)
                    inner = jnp.where(hit, table[j][s][1], inner)
                goes[j, t], its_slot[j, t], its_inner[j, t] = live, slot, inner

    n_slot = n_y - 1
    rank = {}
    code = [[jnp.int32(0)] * n_slot for _ in range(2)]
    for way in range(2):
        for c in range(n_y):
            at = (lambda i: i) if way == 0 else (lambda i: n_y - 1 - i)
            here = [jnp.int32(0)] * n_slot
            count = jnp.int32(0)
            for t in range(n_y - 1, c, -1):
                for j in range(c + 1):
                    pair = (at(j), at(t))
                    rank[way, c, j, t] = count
                    held = its_slot[pair] if j == c else PER + rank[way, c - 1, j, t]
                    for k in range(n_slot):
                        here[k] = jnp.where((goes[pair] == 1) & (count == k), held, here[k])
                    count = count + goes[pair]
            for k in range(n_slot):
                code[way][k] = jnp.where(my_y == at(c), here[k], code[way][k])

    inward = jnp.where(my_y < n_y // 2, 0, 1)
    outward = 1 - inward

    row = lax.broadcasted_iota(jnp.int32, (E, L), 0)
    lane = lax.broadcasted_iota(jnp.int32, (E, L), 1)
    wide_row = lax.broadcasted_iota(jnp.int32, (E // 2, E * E), 0)
    wide_lane = lax.broadcasted_iota(jnp.int32, (E // 2, E * E), 1)
    odd_half = (wide_row + wide_lane // E + wide_lane) % 2 == 1

    fields = ((own_b, st_b, rv_b), (own_u, st_u, rv_u), (own_a, st_a, rv_a), (own_f, st_f, rv_f))
    chunks = (4, 1, 4, 4)

    def part_of(ref, i, way, part):
        if part == chunks[i]:
            return ref.at[way, n_slot - 1]
        rows = ref.shape[2] // chunks[i]
        return ref.at[way, pl.ds(0, n_slot - 1), pl.ds(part * rows, rows)]

    def hop(i, way, part, neighbour):
        _, st, rv = fields[i]
        return pltpu.make_async_remote_copy(
            src_ref=part_of(st, i, way, part),
            dst_ref=part_of(rv, i, way, part),
            send_sem=ms_sem.at[i, way, part],
            recv_sem=mr_sem.at[i, way, part],
            device_id={"gy": neighbour},
            device_id_type=MESH,
        )

    def sends(way):
        return jnp.where(way == 0, my_y < n_y - 1, my_y > 0)

    def receives(way):
        return jnp.where(way == 0, my_y > 0, my_y < n_y - 1)

    def fill(i, way, k, start, rows, relays=True):
        own, st, rv = fields[i]
        held = jnp.where(way == 0, code[0][k], code[1][k])
        slot = jnp.where(held < PER, held, 0)
        if i == 1:
            box = own[slot]
            box = jnp.where(odd_half, box[: E // 2], pltpu.roll(box[E // 2 :], 1, 0))
        else:
            box = own[slot, pl.ds(start, rows), :]
        for r in range(n_slot - 1 if relays else 0):
            relayed = jnp.full((rows, E * E), held, jnp.int32) == PER + r
            box = jnp.where(relayed, rv[way, r, pl.ds(start, rows), :], box)
        st[way, k, pl.ds(start, rows), :] = box

    def take_hop(i, way, part):
        @pl.when(receives(way))
        def _():
            hop(i, way, part, my_y - 1 + 2 * way).wait_recv()

    def pass_on(i, way, part, relays=True):
        @pl.when(sends(way))
        def _():
            rows = fields[i][1].shape[2]
            if part < chunks[i]:
                take_hop(i, way, part)
                rows = rows // chunks[i]
                for k in range(n_slot - 1):
                    fill(i, way, k, part * rows, rows)
            else:
                fill(i, way, n_slot - 1, 0, rows, relays)
            hop(i, way, part, my_y + 1 - 2 * way).start()

    steps = [(i, part) for i in range(4) for part in range(chunks[i] + 1)]
    lag = 2
    ahead = n_y <= 4

    def end_sends(i, parts):
        @pl.when(jnp.logical_not(receives(inward)))
        def _():
            for part in parts:
                pass_on(i, inward, part, relays=False)

    def last_out(i):
        if ahead:
            pass_on(i, outward, chunks[i], relays=False)

    def middle(first_step, last_step):
        @pl.when(receives(inward))
        def _():
            for n in range(first_step, last_step):
                if n < len(steps):
                    pass_on(steps[n][0], inward, steps[n][1])
                if 0 <= n - lag < len(steps):
                    i, part = steps[n - lag]
                    if not (ahead and part == chunks[i]):
                        pass_on(i, outward, part)

    def arrived(i):
        for way in range(2):

            @pl.when(jnp.logical_not(sends(way)))
            def _():
                for part in range(chunks[i]):
                    take_hop(i, way, part)

            take_hop(i, way, chunks[i])

    for i in range(3):
        loaded(i)
        if i == 0:
            pl.semaphore_wait(barrier, partners)
        end_sends(i, range(chunks[i] + 1))
    last_out(0)
    last_out(1)
    middle(0, 7)
    last_out(2)
    middle(7, 11)
    b[...] = jnp.zeros_like(b)
    u[...] = jnp.zeros_like(u)

    own_slot = [jnp.int32(0)] * PER
    is_own = [jnp.int32(0)] * PER
    got_slot = [jnp.int32(0)] * PER
    got_way = [jnp.int32(0)] * PER
    for q in range(PER):
        for s in range(PER):
            owner, inner = owner_inner(my_y, s)
            here = (owner == my_y) & (inner == q)
            own_slot[q] = jnp.where(here, s, own_slot[q])
            is_own[q] = jnp.where(here, 1, is_own[q])
        for way in range(2):
            for t in range(1, n_y):
                for j in range(t):
                    pair = (j, t) if way == 0 else (n_y - 1 - j, n_y - 1 - t)
                    here = (goes[pair] == 1) & (its_inner[pair] == q) & (my_y == pair[1])
                    slot = jnp.minimum(rank[way, t - 1, j, t], n_slot - 1)
                    got_slot[q] = jnp.where(here, slot, got_slot[q])
                    got_way[q] = jnp.where(here, way, got_way[q])

    group = lane // E
    own_mask = [jnp.full((E, L), is_own[q], jnp.int32) == 1 for q in range(PER)]

    def assembled(i, put, carry=0):
        own, _, rv = fields[i]

        def columns(t, carry):
            at = pl.ds(pl.multiple_of(t * L, L), L)
            parts = []
            for q in range(PER):
                got = rv[got_way[q], got_slot[q], :, at]
                if i == 1:
                    got = jnp.concatenate([got, pltpu.roll(got, E // 2 - 1, 0)], axis=0)
                parts.append(jnp.where(own_mask[q], own[own_slot[q], :, at], got))
            for j in range(PER):
                plane = parts[j]
                for q in range(PER):
                    if q != j:
                        plane = jnp.where(
                            group == q, pltpu.roll(parts[q], (q - j) * E % L, 1), plane
                        )
                carry = put(t * PER + j, j, plane, carry)
            return carry

        return lax.fori_loop(0, E * E // L, columns, carry)

    def at_plane(y):
        return pl.ds(pl.multiple_of(y * E, E), E)

    def base(y):
        return pl.multiple_of(y * ST + ST + 8, 8)

    def padded(y):
        return pl.ds(base(y), E)

    even = (row + lane) % 2 == 0
    odd = (row + lane) % 2 == 1
    pair = lane // 2
    zero = jnp.zeros((E, L), jnp.float32)
    first = ST + 8

    def pack_z(y, v, face):
        return jnp.where(pair == y, pltpu.roll(v, 2 * y + 1, 1), face)

    def pack_all_z(ref):
        def planes(t, face):
            for j in range(4):
                y = t * 4 + j
                face = pack_z(y, ref[padded(y), :], face)
            return face

        return lax.fori_loop(0, E // 4, planes, zero)

    def z_halo(e):
        return jnp.where(lane % 2 == 0, hr[e, 4], pltpu.roll(hr[e, 5], L - 2, 1))

    def z_edge(halo, y):
        return pltpu.roll(halo, lax.rem(L - 2 * y, L), 1)

    def face_copy(e, side):
        axis, step = SIDES[side]
        return pltpu.make_async_remote_copy(
            src_ref=hs.at[e, side],
            dst_ref=hr.at[e, side ^ 1],
            send_sem=hs_sem.at[e, side],
            recv_sem=hr_sem.at[e, side ^ 1],
            device_id={axis: me[axis] + step},
            device_id_type=MESH,
        )

    def send_faces(e, ref, z_face):
        hs[e, 0] = ref[pl.ds(first, E, stride=ST), :]
        hs[e, 1] = ref[pl.ds(first + E - 1, E, stride=ST), :]
        hs[e, 2] = ref[pl.ds(first, E), :]
        hs[e, 3] = ref[pl.ds(first + (E - 1) * ST, E), :]
        hs[e, 4] = z_face
        hs[e, 5] = z_face
        for side in range(6):

            @pl.when(exists(side))
            def _():
                face_copy(e, side).start()

    def wait_faces(e):
        for side in range(6):
            axis, step = SIDES[side]

            @pl.when(exists(side))
            def _():
                pltpu.make_async_remote_copy(
                    src_ref=hs.at[e, side],
                    dst_ref=hr.at[e, side],
                    send_sem=hs_sem.at[e, side],
                    recv_sem=hr_sem.at[e, side],
                    device_id={axis: me[axis] + step},
                    device_id_type=MESH,
                ).wait_recv()

    arrived(0)

    def put_b(y, j, plane, carry):
        b[padded(y), :] = plane
        return carry

    assembled(0, put_b)
    send_faces(0, b, pack_all_z(b))

    loaded(3)
    end_sends(3, (0, 1))
    middle(11, 12)

    arrived(1)

    def put_u(y, j, plane, carry):
        u[padded(y), :] = plane
        return carry

    assembled(1, put_u)
    send_faces(1, u, pack_all_z(u))

    end_sends(3, (2, 3, 4))
    last_out(3)
    middle(12, 14)

    wait_faces(0)
    b[pl.ds(first - 1, E, stride=ST), :] = hr[0, 0]
    b[pl.ds(first + E, E, stride=ST), :] = hr[0, 1]
    b[pl.ds(8, E), :] = hr[0, 2]
    b[pl.ds(first + E * ST, E), :] = hr[0, 3]
    b_halo = z_halo(0)

    def coefs(y, carry):
        v = b[padded(y), :]
        at = at_plane(y)
        edge = z_edge(b_halo, y)
        x_low = 0.5 * (b[pl.ds(base(y) - 1, E), :] + v)
        x_high = 0.5 * (b[pl.ds(base(y) + 1, E), :] + v)
        y_low = 0.5 * (b[padded(y - 1), :] + v)
        y_high = 0.5 * (b[padded(y + 1), :] + v)
        z_low = 0.5 * (jnp.where(lane == 0, edge, pltpu.roll(v, 1, 1)) + v)
        z_high = 0.5 * (jnp.where(lane == L - 1, edge, pltpu.roll(v, L - 1, 1)) + v)
        cxl[at, :] = x_low
        cxh[at, :] = x_high
        cy[at, :] = y_low
        cy[at_plane(y + 1), :] = y_high
        czl[at, :] = jnp.where(lane == 0, 0.0, z_low)
        czh[at, :] = jnp.where(lane == L - 1, 0.0, z_high)
        ez[at, :] = jnp.where(lane == 0, z_low, jnp.where(lane == L - 1, z_high, 0.0))
        dia[at, :] = (x_high + x_low) + (y_high + y_low) + (z_high + z_low)
        return carry

    lax.fori_loop(0, E, coefs, 0)

    middle(14, 16)
    arrived(2)

    def put_a(y, j, plane, carry):
        at = at_plane(y)
        total = plane + dia[at, :]
        inverse = 1.0 / total
        dia[at, :] = total
        inv[at, :] = inverse
        ezi[at, :] = ez[at, :] * inverse
        return carry

    assembled(2, put_a)

    def neighbours(y):
        at = at_plane(y)
        v = u[padded(y), :]
        x_sum = cxh[at, :] * u[pl.ds(base(y) + 1, E), :] + cxl[at, :] * u[pl.ds(base(y) - 1, E), :]
        y_sum = cy[at_plane(y + 1), :] * u[padded(y + 1), :] + cy[at, :] * u[padded(y - 1), :]
        z_sum = czh[at, :] * pltpu.roll(v, L - 1, 1) + czl[at, :] * pltpu.roll(v, 1, 1)
        return v, x_sum + y_sum + z_sum

    low_x = pl.ds(0, E, stride=E)
    high_x = pl.ds(E - 1, E, stride=E)
    low_y = pl.ds(0, E)
    high_y = pl.ds((E - 1) * E, E)
    top_y = pl.ds(E * E, E)

    def add_faces(e):
        for at, term in (
            (low_x, cxl[low_x, :] * hr[e, 0]),
            (high_x, cxh[high_x, :] * hr[e, 1]),
            (low_y, cy[low_y, :] * hr[e, 2]),
            (high_y, cy[top_y, :] * hr[e, 3]),
        ):
            res[at, :] = res[at, :] + term

    middle(16, len(steps) + lag)
    wait_faces(1)
    first_halo = z_halo(1)

    def first_sums(t, carry):
        for j in range(4):
            y = t * 4 + j
            at = at_plane(y)
            res[at, :] = neighbours(y)[1] + ez[at, :] * z_edge(first_halo, y)
        return carry

    lax.fori_loop(0, E // 4, first_sums, 0)
    add_faces(1)
    arrived(3)

    def put_f(y, j, plane, face):
        at = at_plane(y)
        f[at, :] = plane
        new = (plane + res[at, :]) * inv[at, :]
        v = jnp.where(even if j % 2 == 0 else odd, new, u[padded(y), :])
        u[padded(y), :] = v
        return pack_z(y, v, face)

    send_faces(2, u, assembled(3, put_f, zero))

    e = 2
    for sweep in range(SWEEPS):
        for colour in (0, 1):
            if sweep == 0 and colour == 0:
                continue
            masks = (even, odd) if colour == 0 else (odd, even)

            def planes(t, carry):
                for j in range(4):
                    y = t * 4 + j
                    at = at_plane(y)
                    v, total = neighbours(y)
                    new = (f[at, :] + total) * inv[at, :]
                    u[padded(y), :] = jnp.where(masks[j % 2], new, v)
                return carry

            lax.fori_loop(0, E // 4, planes, 0)
            wait_faces(e)
            for at, mask, term in (
                (pl.ds(first, E, stride=ST), 0, cxl[low_x, :] * inv[low_x, :] * hr[e, 0]),
                (pl.ds(first + E - 1, E, stride=ST), 1, cxh[high_x, :] * inv[high_x, :] * hr[e, 1]),
                (pl.ds(first, E), 0, cy[low_y, :] * inv[low_y, :] * hr[e, 2]),
                (pl.ds(first + (E - 1) * ST, E), 1, cy[top_y, :] * inv[high_y, :] * hr[e, 3]),
            ):
                u[at, :] = u[at, :] + jnp.where(masks[mask], term, 0.0)
            halo = z_halo(e)

            def edges(t, face):
                for j in range(4):
                    y = t * 4 + j
                    term = ezi[at_plane(y), :] * z_edge(halo, y)
                    v = u[padded(y), :] + jnp.where(masks[j % 2], term, 0.0)
                    u[padded(y), :] = v
                    face = pack_z(y, v, face)
                return face

            face = lax.fori_loop(0, E // 4, edges, zero)
            e += 1
            send_faces(e, u, face)

    def residual(t, carry):
        for j in range(4):
            y = t * 4 + j
            at = at_plane(y)
            v, total = neighbours(y)
            res[at, :] = f[at, :] - (dia[at, :] * v - total)
        return carry

    lax.fori_loop(0, E // 4, residual, 0)
    for x in range(E):
        sol_out[x] = u[pl.ds(first + x, E, stride=ST), :]
    wait_faces(e)
    add_faces(e)
    last_halo = z_halo(e)

    def last_edges(t, carry):
        for j in range(4):
            y = t * 4 + j
            at = at_plane(y)
            res[at, :] = res[at, :] + ez[at, :] * z_edge(last_halo, y)
        return carry

    lax.fori_loop(0, E // 4, last_edges, 0)
    for x in range(E):
        res_out[x] = res[pl.ds(x, E, stride=E), :]

    for i, part in steps:
        for way in range(2):

            @pl.when(sends(way))
            def _():
                hop(i, way, part, my_y + 1 - 2 * way).wait_send()

    for exchange in range(e + 1):
        for side in range(6):

            @pl.when(exists(side))
            def _():
                face_copy(exchange, side).wait_send()


def per_device(width, solution_old, right_side, acoef, bcoef, corners):
    n_y = width["gy"]
    exchanges = 2 + 2 * SWEEPS
    box = (E, E * E)
    field = pltpu.VMEM((E * E, L), jnp.float32)
    padded = pltpu.VMEM(((E + 2) * ST + 16, L), jnp.float32)
    faces = pltpu.VMEM((exchanges, 6, E, L), jnp.float32)
    own = pltpu.VMEM((PER,) + box, jnp.float32)
    moved = pltpu.VMEM((2, n_y - 1) + box, jnp.float32)
    half = pltpu.VMEM((2, n_y - 1, E // 2, E * E), jnp.float32)
    out = jax.ShapeDtypeStruct((E, E, L), jnp.float32)
    return pl.pallas_call(
        functools.partial(kernel, width),
        out_shape=(out, out),
        in_specs=[pl.BlockSpec(memory_space=pltpu.SMEM)]
        + [pl.BlockSpec(memory_space=pl.ANY)] * 4,
        out_specs=(pl.BlockSpec(memory_space=pltpu.VMEM),) * 2,
        scratch_shapes=[own] * 4
        + [moved, half, moved, moved] * 2
        + [padded, padded]
        + [field] * 6
        + [pltpu.VMEM(((E + 1) * E, L), jnp.float32)]
        + [field] * 4
        + [faces] * 2
        + [
            pltpu.SemaphoreType.DMA((4, PER)),
            pltpu.SemaphoreType.DMA((4, 2, 5)),
            pltpu.SemaphoreType.DMA((4, 2, 5)),
            pltpu.SemaphoreType.DMA((exchanges, 6)),
            pltpu.SemaphoreType.DMA((exchanges, 6)),
        ],
        compiler_params=pltpu.CompilerParams(
            collective_id=0, has_side_effects=True, vmem_limit_bytes=64 * 1024 * 1024
        ),
        cost_estimate=pl.CostEstimate(
            flops=100 * E * E * L, bytes_accessed=24 * E * E * L, transcendentals=0
        ),
    )(corners, solution_old, right_side, acoef, bcoef)


def solution(mesh):
    width = dict(mesh.shape)
    boxes = P(("gx", "gy", "gz"), None, None)
    level = P("gx", "gy", "gz")
    return jax.shard_map(
        functools.partial(per_device, width),
        mesh=mesh,
        in_specs=(boxes, boxes, boxes, boxes, P()),
        out_specs=(level, level),
        check_vma=False,
    )
```

```python
import functools

import jax
import jax.numpy as jnp
from jax import lax
from jax.experimental import pallas as pl
from jax.experimental.pallas import tpu as pltpu
from jax.sharding import PartitionSpec as P

SWEEPS = 2
E = 32
L = 128
PER = 4
ST = E + 8
MESH = pl.DeviceIdType.MESH
SIDES = (("gx", -1), ("gx", 1), ("gy", -1), ("gy", 1), ("gz", -1), ("gz", 1))


def kernel(
    width,
    corners,
    sol_in,
    rhs_in,
    abs_in,
    dif_in,
    sol_hbm,
    res_hbm,
    own_b,
    own_u,
    own_a,
    own_f,
    st_b,
    st_u,
    st_a,
    st_f,
    rv_b,
    rv_u,
    rv_a,
    rv_f,
    b,
    u,
    f,
    dia,
    inv,
    res,
    cxl,
    cxh,
    cy,
    czl,
    czh,
    ez,
    ezi,
    hs,
    hr,
    sol_out,
    res_out,
    out_sem,
    in_sem,
    ms_sem,
    mr_sem,
    hs_sem,
    hr_sem,
):
    me = {axis: lax.axis_index(axis) for axis in ("gx", "gy", "gz")}
    n_y = width["gy"]
    my_y = me["gy"]

    loads = [
        [
            pltpu.make_async_copy(src.at[q], dst.at[q], in_sem.at[i, q])
            for q in range(PER)
        ]
        for i, (src, dst) in enumerate(
            ((dif_in, own_b), (sol_in, own_u), (abs_in, own_a), (rhs_in, own_f))
        )
    ]
    for field_loads in loads:
        for load in field_loads:
            load.start()

    def loaded(i):
        for load in loads[i]:
            load.wait()

    def exists(side):
        axis, step = SIDES[side]
        return me[axis] > 0 if step < 0 else me[axis] < width[axis] - 1

    hr[...] = jnp.zeros_like(hr)

    barrier = pltpu.get_barrier_semaphore()
    partners = 0
    for side in range(6):
        axis, step = SIDES[side]

        @pl.when(exists(side))
        def _():
            pl.semaphore_signal(
                barrier, inc=1, device_id={axis: me[axis] + step}, device_id_type=MESH
            )

        partners = partners + exists(side).astype(jnp.int32)

    def owner_inner(device, slot):
        row = ((me["gx"] * n_y + device) * width["gz"] + me["gz"]) * PER + slot
        return lax.div(corners[1, row], E), lax.div(lax.rem(corners[2, row], PER * E), E)

    table = [[owner_inner(j, s) for s in range(PER)] for j in range(n_y)]
    goes, its_slot, its_inner = {}, {}, {}
    for j in range(n_y):
        for t in range(n_y):
            if t != j:
                live, slot, inner = jnp.int32(0), jnp.int32(0), jnp.int32(0)
                for s in range(PER):
                    hit = table[j][s][0] == t
                    live = jnp.where(hit, 1, live)
                    slot = jnp.where(hit, s, slot)
                    inner = jnp.where(hit, table[j][s][1], inner)
                goes[j, t], its_slot[j, t], its_inner[j, t] = live, slot, inner

    n_slot = n_y - 1
    rank = {}
    code = [[jnp.int32(0)] * n_slot for _ in range(2)]
    for way in range(2):
        for c in range(n_y):
            at = (lambda i: i) if way == 0 else (lambda i: n_y - 1 - i)
            here = [jnp.int32(0)] * n_slot
            count = jnp.int32(0)
            for t in range(n_y - 1, c, -1):
                for j in range(c + 1):
                    pair = (at(j), at(t))
                    rank[way, c, j, t] = count
                    held = its_slot[pair] if j == c else PER + rank[way, c - 1, j, t]
                    for k in range(n_slot):
                        here[k] = jnp.where((goes[pair] == 1) & (count == k), held, here[k])
                    count = count + goes[pair]
            for k in range(n_slot):
                code[way][k] = jnp.where(my_y == at(c), here[k], code[way][k])

    inward = jnp.where(my_y < n_y // 2, 0, 1)
    outward = 1 - inward

    row = lax.broadcasted_iota(jnp.int32, (E, L), 0)
    lane = lax.broadcasted_iota(jnp.int32, (E, L), 1)
    wide_row = lax.broadcasted_iota(jnp.int32, (E // 2, E * E), 0)
    wide_lane = lax.broadcasted_iota(jnp.int32, (E // 2, E * E), 1)
    odd_half = (wide_row + wide_lane // E + wide_lane) % 2 == 1

    fields = ((own_b, st_b, rv_b), (own_u, st_u, rv_u), (own_a, st_a, rv_a), (own_f, st_f, rv_f))
    chunks = (4, 1, 4, 4)

    def part_of(ref, i, way, part):
        if part == chunks[i]:
            return ref.at[way, n_slot - 1]
        rows = ref.shape[2] // chunks[i]
        return ref.at[way, pl.ds(0, n_slot - 1), pl.ds(part * rows, rows)]

    def hop(i, way, part, neighbour):
        _, st, rv = fields[i]
        return pltpu.make_async_remote_copy(
            src_ref=part_of(st, i, way, part),
            dst_ref=part_of(rv, i, way, part),
            send_sem=ms_sem.at[i, way, part],
            recv_sem=mr_sem.at[i, way, part],
            device_id={"gy": neighbour},
            device_id_type=MESH,
        )

    def sends(way):
        return jnp.where(way == 0, my_y < n_y - 1, my_y > 0)

    def receives(way):
        return jnp.where(way == 0, my_y > 0, my_y < n_y - 1)

    def fill(i, way, k, start, rows, relays=True):
        own, st, rv = fields[i]
        held = jnp.where(way == 0, code[0][k], code[1][k])
        slot = jnp.where(held < PER, held, 0)
        if i == 1:
            box = own[slot]
            box = jnp.where(odd_half, box[: E // 2], pltpu.roll(box[E // 2 :], 1, 0))
        else:
            box = own[slot, pl.ds(start, rows), :]
        for r in range(n_slot - 1 if relays else 0):
            relayed = jnp.full((rows, E * E), held, jnp.int32) == PER + r
            box = jnp.where(relayed, rv[way, r, pl.ds(start, rows), :], box)
        st[way, k, pl.ds(start, rows), :] = box

    def take_hop(i, way, part):
        @pl.when(receives(way))
        def _():
            hop(i, way, part, my_y - 1 + 2 * way).wait_recv()

    def pass_on(i, way, part, relays=True):
        @pl.when(sends(way))
        def _():
            rows = fields[i][1].shape[2]
            if part < chunks[i]:
                take_hop(i, way, part)
                rows = rows // chunks[i]
                for k in range(n_slot - 1):
                    fill(i, way, k, part * rows, rows)
            else:
                fill(i, way, n_slot - 1, 0, rows, relays)
            hop(i, way, part, my_y + 1 - 2 * way).start()

    steps = [(i, part) for i in range(4) for part in range(chunks[i] + 1)]
    lag = 2
    ahead = n_y <= 4

    def end_sends(i, parts):
        @pl.when(jnp.logical_not(receives(inward)))
        def _():
            for part in parts:
                pass_on(i, inward, part, relays=False)

    def last_out(i):
        if ahead:
            pass_on(i, outward, chunks[i], relays=False)

    def middle(first_step, last_step):
        @pl.when(receives(inward))
        def _():
            for n in range(first_step, last_step):
                if n < len(steps):
                    pass_on(steps[n][0], inward, steps[n][1])
                if 0 <= n - lag < len(steps):
                    i, part = steps[n - lag]
                    if not (ahead and part == chunks[i]):
                        pass_on(i, outward, part)

    def arrived(i):
        for way in range(2):

            @pl.when(jnp.logical_not(sends(way)))
            def _():
                for part in range(chunks[i]):
                    take_hop(i, way, part)

            take_hop(i, way, chunks[i])

    for i in range(3):
        loaded(i)
        if i == 0:
            pl.semaphore_wait(barrier, partners)
        end_sends(i, range(chunks[i] + 1))
    last_out(0)
    last_out(1)
    middle(0, 7)
    last_out(2)
    middle(7, 11)
    b[...] = jnp.zeros_like(b)
    u[...] = jnp.zeros_like(u)

    own_slot = [jnp.int32(0)] * PER
    is_own = [jnp.int32(0)] * PER
    got_slot = [jnp.int32(0)] * PER
    got_way = [jnp.int32(0)] * PER
    for q in range(PER):
        for s in range(PER):
            owner, inner = owner_inner(my_y, s)
            here = (owner == my_y) & (inner == q)
            own_slot[q] = jnp.where(here, s, own_slot[q])
            is_own[q] = jnp.where(here, 1, is_own[q])
        for way in range(2):
            for t in range(1, n_y):
                for j in range(t):
                    pair = (j, t) if way == 0 else (n_y - 1 - j, n_y - 1 - t)
                    here = (goes[pair] == 1) & (its_inner[pair] == q) & (my_y == pair[1])
                    slot = jnp.minimum(rank[way, t - 1, j, t], n_slot - 1)
                    got_slot[q] = jnp.where(here, slot, got_slot[q])
                    got_way[q] = jnp.where(here, way, got_way[q])

    group = lane // E
    own_mask = [jnp.full((E, L), is_own[q], jnp.int32) == 1 for q in range(PER)]

    def assembled(i, put, carry=0):
        own, _, rv = fields[i]

        def columns(t, carry):
            at = pl.ds(pl.multiple_of(t * L, L), L)
            parts = []
            for q in range(PER):
                got = rv[got_way[q], got_slot[q], :, at]
                if i == 1:
                    got = jnp.concatenate([got, pltpu.roll(got, E // 2 - 1, 0)], axis=0)
                parts.append(jnp.where(own_mask[q], own[own_slot[q], :, at], got))
            for j in range(PER):
                plane = parts[j]
                for q in range(PER):
                    if q != j:
                        plane = jnp.where(
                            group == q, pltpu.roll(parts[q], (q - j) * E % L, 1), plane
                        )
                carry = put(t * PER + j, j, plane, carry)
            return carry

        return lax.fori_loop(0, E * E // L, columns, carry)

    def at_plane(y):
        return pl.ds(pl.multiple_of(y * E, E), E)

    def base(y):
        return pl.multiple_of(y * ST + ST + 8, 8)

    def padded(y):
        return pl.ds(base(y), E)

    even = (row + lane) % 2 == 0
    odd = (row + lane) % 2 == 1
    pair = lane // 2
    zero = jnp.zeros((E, L), jnp.float32)
    first = ST + 8

    def pack_z(y, v, face):
        return jnp.where(pair == y, pltpu.roll(v, 2 * y + 1, 1), face)

    def pack_all_z(ref):
        def planes(t, face):
            for j in range(4):
                y = t * 4 + j
                face = pack_z(y, ref[padded(y), :], face)
            return face

        return lax.fori_loop(0, E // 4, planes, zero)

    def z_halo(e):
        return jnp.where(lane % 2 == 0, hr[e, 4], pltpu.roll(hr[e, 5], L - 2, 1))

    def z_edge(halo, y):
        return pltpu.roll(halo, lax.rem(L - 2 * y, L), 1)

    def face_copy(e, side):
        axis, step = SIDES[side]
        return pltpu.make_async_remote_copy(
            src_ref=hs.at[e, side],
            dst_ref=hr.at[e, side ^ 1],
            send_sem=hs_sem.at[e, side],
            recv_sem=hr_sem.at[e, side ^ 1],
            device_id={axis: me[axis] + step},
            device_id_type=MESH,
        )

    def send_faces(e, ref, z_face):
        hs[e, 0] = ref[pl.ds(first, E, stride=ST), :]
        hs[e, 1] = ref[pl.ds(first + E - 1, E, stride=ST), :]
        hs[e, 2] = ref[pl.ds(first, E), :]
        hs[e, 3] = ref[pl.ds(first + (E - 1) * ST, E), :]
        hs[e, 4] = z_face
        hs[e, 5] = z_face
        for side in range(6):

            @pl.when(exists(side))
            def _():
                face_copy(e, side).start()

    def wait_faces(e):
        for side in range(6):
            axis, step = SIDES[side]

            @pl.when(exists(side))
            def _():
                pltpu.make_async_remote_copy(
                    src_ref=hs.at[e, side],
                    dst_ref=hr.at[e, side],
                    send_sem=hs_sem.at[e, side],
                    recv_sem=hr_sem.at[e, side],
                    device_id={axis: me[axis] + step},
                    device_id_type=MESH,
                ).wait_recv()

    arrived(0)

    def put_b(y, j, plane, carry):
        b[padded(y), :] = plane
        return carry

    assembled(0, put_b)
    send_faces(0, b, pack_all_z(b))

    loaded(3)
    end_sends(3, (0, 1))
    middle(11, 12)

    arrived(1)

    def put_u(y, j, plane, carry):
        u[padded(y), :] = plane
        return carry

    assembled(1, put_u)
    send_faces(1, u, pack_all_z(u))

    end_sends(3, (2, 3, 4))
    last_out(3)
    middle(12, 14)

    wait_faces(0)
    b[pl.ds(first - 1, E, stride=ST), :] = hr[0, 0]
    b[pl.ds(first + E, E, stride=ST), :] = hr[0, 1]
    b[pl.ds(8, E), :] = hr[0, 2]
    b[pl.ds(first + E * ST, E), :] = hr[0, 3]
    b_halo = z_halo(0)

    def coefs(y, carry):
        v = b[padded(y), :]
        at = at_plane(y)
        edge = z_edge(b_halo, y)
        x_low = 0.5 * (b[pl.ds(base(y) - 1, E), :] + v)
        x_high = 0.5 * (b[pl.ds(base(y) + 1, E), :] + v)
        y_low = 0.5 * (b[padded(y - 1), :] + v)
        y_high = 0.5 * (b[padded(y + 1), :] + v)
        z_low = 0.5 * (jnp.where(lane == 0, edge, pltpu.roll(v, 1, 1)) + v)
        z_high = 0.5 * (jnp.where(lane == L - 1, edge, pltpu.roll(v, L - 1, 1)) + v)
        cxl[at, :] = x_low
        cxh[at, :] = x_high
        cy[at, :] = y_low
        cy[at_plane(y + 1), :] = y_high
        czl[at, :] = jnp.where(lane == 0, 0.0, z_low)
        czh[at, :] = jnp.where(lane == L - 1, 0.0, z_high)
        ez[at, :] = jnp.where(lane == 0, z_low, jnp.where(lane == L - 1, z_high, 0.0))
        dia[at, :] = (x_high + x_low) + (y_high + y_low) + (z_high + z_low)
        return carry

    lax.fori_loop(0, E, coefs, 0)

    middle(14, 16)
    arrived(2)

    def put_a(y, j, plane, carry):
        at = at_plane(y)
        total = plane + dia[at, :]
        inverse = 1.0 / total
        dia[at, :] = total
        inv[at, :] = inverse
        ezi[at, :] = ez[at, :] * inverse
        return carry

    assembled(2, put_a)

    def neighbours(y):
        at = at_plane(y)
        v = u[padded(y), :]
        x_sum = cxh[at, :] * u[pl.ds(base(y) + 1, E), :] + cxl[at, :] * u[pl.ds(base(y) - 1, E), :]
        y_sum = cy[at_plane(y + 1), :] * u[padded(y + 1), :] + cy[at, :] * u[padded(y - 1), :]
        z_sum = czh[at, :] * pltpu.roll(v, L - 1, 1) + czl[at, :] * pltpu.roll(v, 1, 1)
        return v, x_sum + y_sum + z_sum

    low_x = pl.ds(0, E, stride=E)
    high_x = pl.ds(E - 1, E, stride=E)
    low_y = pl.ds(0, E)
    high_y = pl.ds((E - 1) * E, E)
    top_y = pl.ds(E * E, E)

    def add_faces(e):
        for at, term in (
            (low_x, cxl[low_x, :] * hr[e, 0]),
            (high_x, cxh[high_x, :] * hr[e, 1]),
            (low_y, cy[low_y, :] * hr[e, 2]),
            (high_y, cy[top_y, :] * hr[e, 3]),
        ):
            res[at, :] = res[at, :] + term

    middle(16, len(steps) + lag)
    wait_faces(1)
    first_halo = z_halo(1)

    def first_sums(t, carry):
        for j in range(4):
            y = t * 4 + j
            at = at_plane(y)
            res[at, :] = neighbours(y)[1] + ez[at, :] * z_edge(first_halo, y)
        return carry

    lax.fori_loop(0, E // 4, first_sums, 0)
    add_faces(1)
    arrived(3)

    def put_f(y, j, plane, face):
        at = at_plane(y)
        f[at, :] = plane
        new = (plane + res[at, :]) * inv[at, :]
        v = jnp.where(even if j % 2 == 0 else odd, new, u[padded(y), :])
        u[padded(y), :] = v
        return pack_z(y, v, face)

    send_faces(2, u, assembled(3, put_f, zero))

    e = 2
    for sweep in range(SWEEPS):
        for colour in (0, 1):
            if sweep == 0 and colour == 0:
                continue
            masks = (even, odd) if colour == 0 else (odd, even)

            def planes(t, carry):
                for j in range(4):
                    y = t * 4 + j
                    at = at_plane(y)
                    v, total = neighbours(y)
                    new = (f[at, :] + total) * inv[at, :]
                    u[padded(y), :] = jnp.where(masks[j % 2], new, v)
                return carry

            lax.fori_loop(0, E // 4, planes, 0)
            wait_faces(e)
            for at, mask, term in (
                (pl.ds(first, E, stride=ST), 0, cxl[low_x, :] * inv[low_x, :] * hr[e, 0]),
                (pl.ds(first + E - 1, E, stride=ST), 1, cxh[high_x, :] * inv[high_x, :] * hr[e, 1]),
                (pl.ds(first, E), 0, cy[low_y, :] * inv[low_y, :] * hr[e, 2]),
                (pl.ds(first + (E - 1) * ST, E), 1, cy[top_y, :] * inv[high_y, :] * hr[e, 3]),
            ):
                u[at, :] = u[at, :] + jnp.where(masks[mask], term, 0.0)
            halo = z_halo(e)

            def edges(t, face):
                for j in range(4):
                    y = t * 4 + j
                    term = ezi[at_plane(y), :] * z_edge(halo, y)
                    v = u[padded(y), :] + jnp.where(masks[j % 2], term, 0.0)
                    u[padded(y), :] = v
                    face = pack_z(y, v, face)
                return face

            face = lax.fori_loop(0, E // 4, edges, zero)
            e += 1
            send_faces(e, u, face)

    def residual(t, carry):
        for j in range(4):
            y = t * 4 + j
            at = at_plane(y)
            v, total = neighbours(y)
            res[at, :] = f[at, :] - (dia[at, :] * v - total)
        return carry

    lax.fori_loop(0, E // 4, residual, 0)
    for x in range(E):
        sol_out[x] = u[pl.ds(first + x, E, stride=ST), :]
    stores = [pltpu.make_async_copy(sol_out, sol_hbm, out_sem.at[4])]
    stores[0].start()
    wait_faces(e)
    add_faces(e)
    last_halo = z_halo(e)

    def last_edges(t, carry):
        for j in range(4):
            y = t * 4 + j
            at = at_plane(y)
            res[at, :] = res[at, :] + ez[at, :] * z_edge(last_halo, y)
        return carry

    lax.fori_loop(0, E // 4, last_edges, 0)
    for x in range(E):
        res_out[x] = res[pl.ds(x, E, stride=E), :]
        if x % 8 == 7:
            piece = pl.ds(x - 7, 8)
            stores.append(
                pltpu.make_async_copy(res_out.at[piece], res_hbm.at[piece], out_sem.at[x // 8])
            )
            stores[-1].start()

    for i, part in steps:
        for way in range(2):

            @pl.when(sends(way))
            def _():
                hop(i, way, part, my_y + 1 - 2 * way).wait_send()

    for store in stores:
        store.wait()

    for exchange in range(e + 1):
        for side in range(6):

            @pl.when(exists(side))
            def _():
                face_copy(exchange, side).wait_send()


def per_device(width, solution_old, right_side, acoef, bcoef, corners):
    n_y = width["gy"]
    exchanges = 2 + 2 * SWEEPS
    box = (E, E * E)
    field = pltpu.VMEM((E * E, L), jnp.float32)
    padded = pltpu.VMEM(((E + 2) * ST + 16, L), jnp.float32)
    faces = pltpu.VMEM((exchanges, 6, E, L), jnp.float32)
    own = pltpu.VMEM((PER,) + box, jnp.float32)
    moved = pltpu.VMEM((2, n_y - 1) + box, jnp.float32)
    half = pltpu.VMEM((2, n_y - 1, E // 2, E * E), jnp.float32)
    out = jax.ShapeDtypeStruct((E, E, L), jnp.float32)
    return pl.pallas_call(
        functools.partial(kernel, width),
        out_shape=(out, out),
        in_specs=[pl.BlockSpec(memory_space=pltpu.SMEM)]
        + [pl.BlockSpec(memory_space=pl.ANY)] * 4,
        out_specs=(pl.BlockSpec(memory_space=pl.ANY),) * 2,
        scratch_shapes=[own] * 4
        + [moved, half, moved, moved] * 2
        + [padded, padded]
        + [field] * 6
        + [pltpu.VMEM(((E + 1) * E, L), jnp.float32)]
        + [field] * 4
        + [faces] * 2
        + [pltpu.VMEM((E, E, L), jnp.float32)] * 2
        + [pltpu.SemaphoreType.DMA((5,))]
        + [
            pltpu.SemaphoreType.DMA((4, PER)),
            pltpu.SemaphoreType.DMA((4, 2, 5)),
            pltpu.SemaphoreType.DMA((4, 2, 5)),
            pltpu.SemaphoreType.DMA((exchanges, 6)),
            pltpu.SemaphoreType.DMA((exchanges, 6)),
        ],
        compiler_params=pltpu.CompilerParams(
            collective_id=0, has_side_effects=True, vmem_limit_bytes=64 * 1024 * 1024
        ),
        cost_estimate=pl.CostEstimate(
            flops=100 * E * E * L, bytes_accessed=24 * E * E * L, transcendentals=0
        ),
    )(corners, solution_old, right_side, acoef, bcoef)


def solution(mesh):
    width = dict(mesh.shape)
    boxes = P(("gx", "gy", "gz"), None, None)
    level = P("gx", "gy", "gz")
    return jax.shard_map(
        functools.partial(per_device, width),
        mesh=mesh,
        in_specs=(boxes, boxes, boxes, boxes, P()),
        out_specs=(level, level),
        check_vma=False,
    )
```

```python
import functools

import jax
import jax.numpy as jnp
from jax import lax
from jax.experimental import pallas as pl
from jax.experimental.pallas import tpu as pltpu
from jax.sharding import PartitionSpec as P

SWEEPS = 2
E = 32
L = 128
PER = 4
ST = E + 8
MESH = pl.DeviceIdType.MESH
SIDES = (("gx", -1), ("gx", 1), ("gy", -1), ("gy", 1), ("gz", -1), ("gz", 1))


def kernel(
    width,
    corners,
    sol_in,
    rhs_in,
    abs_in,
    dif_in,
    sol_hbm,
    res_hbm,
    own_b,
    own_u,
    own_a,
    own_f,
    st_b,
    st_u,
    st_a,
    st_f,
    rv_b,
    rv_u,
    rv_a,
    rv_f,
    b,
    u,
    f,
    dia,
    inv,
    res,
    cxl,
    cxh,
    cy,
    czl,
    czh,
    ez,
    ezi,
    hs,
    hr,
    sol_out,
    res_out,
    out_sem,
    in_sem,
    ms_sem,
    mr_sem,
    hs_sem,
    hr_sem,
):
    me = {axis: lax.axis_index(axis) for axis in ("gx", "gy", "gz")}
    n_y = width["gy"]
    my_y = me["gy"]

    loads = [
        [
            pltpu.make_async_copy(src.at[q], dst.at[q], in_sem.at[i, q])
            for q in range(PER)
        ]
        for i, (src, dst) in enumerate(
            ((dif_in, own_b), (sol_in, own_u), (abs_in, own_a), (rhs_in, own_f))
        )
    ]
    for field_loads in loads:
        for load in field_loads:
            load.start()

    def loaded(i):
        for load in loads[i]:
            load.wait()

    def exists(side):
        axis, step = SIDES[side]
        return me[axis] > 0 if step < 0 else me[axis] < width[axis] - 1

    hr[...] = jnp.zeros_like(hr)

    barrier = pltpu.get_barrier_semaphore()
    partners = 0
    for side in range(6):
        axis, step = SIDES[side]

        @pl.when(exists(side))
        def _():
            pl.semaphore_signal(
                barrier, inc=1, device_id={axis: me[axis] + step}, device_id_type=MESH
            )

        partners = partners + exists(side).astype(jnp.int32)

    def owner_inner(device, slot):
        row = ((me["gx"] * n_y + device) * width["gz"] + me["gz"]) * PER + slot
        return lax.div(corners[1, row], E), lax.div(lax.rem(corners[2, row], PER * E), E)

    table = [[owner_inner(j, s) for s in range(PER)] for j in range(n_y)]
    goes, its_slot, its_inner = {}, {}, {}
    for j in range(n_y):
        for t in range(n_y):
            if t != j:
                live, slot, inner = jnp.int32(0), jnp.int32(0), jnp.int32(0)
                for s in range(PER):
                    hit = table[j][s][0] == t
                    live = jnp.where(hit, 1, live)
                    slot = jnp.where(hit, s, slot)
                    inner = jnp.where(hit, table[j][s][1], inner)
                goes[j, t], its_slot[j, t], its_inner[j, t] = live, slot, inner

    n_slot = n_y - 1
    rank = {}
    code = [[jnp.int32(0)] * n_slot for _ in range(2)]
    for way in range(2):
        for c in range(n_y):
            at = (lambda i: i) if way == 0 else (lambda i: n_y - 1 - i)
            here = [jnp.int32(0)] * n_slot
            count = jnp.int32(0)
            for t in range(n_y - 1, c, -1):
                for j in range(c + 1):
                    pair = (at(j), at(t))
                    rank[way, c, j, t] = count
                    held = its_slot[pair] if j == c else PER + rank[way, c - 1, j, t]
                    for k in range(n_slot):
                        here[k] = jnp.where((goes[pair] == 1) & (count == k), held, here[k])
                    count = count + goes[pair]
            for k in range(n_slot):
                code[way][k] = jnp.where(my_y == at(c), here[k], code[way][k])

    inward = jnp.where(my_y < n_y // 2, 0, 1)
    outward = 1 - inward

    row = lax.broadcasted_iota(jnp.int32, (E, L), 0)
    lane = lax.broadcasted_iota(jnp.int32, (E, L), 1)
    wide_row = lax.broadcasted_iota(jnp.int32, (E // 2, E * E), 0)
    wide_lane = lax.broadcasted_iota(jnp.int32, (E // 2, E * E), 1)
    odd_half = (wide_row + wide_lane // E + wide_lane) % 2 == 1

    fields = ((own_b, st_b, rv_b), (own_u, st_u, rv_u), (own_a, st_a, rv_a), (own_f, st_f, rv_f))
    chunks = (4, 1, 4, 4)

    def part_of(ref, i, way, part):
        if part == chunks[i]:
            return ref.at[way, n_slot - 1]
        rows = ref.shape[2] // chunks[i]
        return ref.at[way, pl.ds(0, n_slot - 1), pl.ds(part * rows, rows)]

    def hop(i, way, part, neighbour):
        _, st, rv = fields[i]
        return pltpu.make_async_remote_copy(
            src_ref=part_of(st, i, way, part),
            dst_ref=part_of(rv, i, way, part),
            send_sem=ms_sem.at[i, way, part],
            recv_sem=mr_sem.at[i, way, part],
            device_id={"gy": neighbour},
            device_id_type=MESH,
        )

    def sends(way):
        return jnp.where(way == 0, my_y < n_y - 1, my_y > 0)

    def receives(way):
        return jnp.where(way == 0, my_y > 0, my_y < n_y - 1)

    def fill(i, way, k, start, rows, relays=True):
        own, st, rv = fields[i]
        held = jnp.where(way == 0, code[0][k], code[1][k])
        slot = jnp.where(held < PER, held, 0)
        if i == 1:
            box = own[slot]
            box = jnp.where(odd_half, box[: E // 2], pltpu.roll(box[E // 2 :], 1, 0))
        else:
            box = own[slot, pl.ds(start, rows), :]
        for r in range(n_slot - 1 if relays else 0):
            relayed = jnp.full((rows, E * E), held, jnp.int32) == PER + r
            box = jnp.where(relayed, rv[way, r, pl.ds(start, rows), :], box)
        st[way, k, pl.ds(start, rows), :] = box

    def take_hop(i, way, part):
        @pl.when(receives(way))
        def _():
            hop(i, way, part, my_y - 1 + 2 * way).wait_recv()

    def pass_on(i, way, part, relays=True):
        @pl.when(sends(way))
        def _():
            rows = fields[i][1].shape[2]
            if part < chunks[i]:
                take_hop(i, way, part)
                rows = rows // chunks[i]
                for k in range(n_slot - 1):
                    fill(i, way, k, part * rows, rows)
            else:
                fill(i, way, n_slot - 1, 0, rows, relays)
            hop(i, way, part, my_y + 1 - 2 * way).start()

    steps = [(i, part) for i in range(4) for part in range(chunks[i] + 1)]
    lag = 1
    ahead = n_y <= 4

    def end_sends(i, parts):
        @pl.when(jnp.logical_not(receives(inward)))
        def _():
            for part in parts:
                pass_on(i, inward, part, relays=False)

    def last_out(i):
        if ahead:
            pass_on(i, outward, chunks[i], relays=False)

    def middle(first_step, last_step):
        @pl.when(receives(inward))
        def _():
            for n in range(first_step, last_step):
                if n < len(steps):
                    pass_on(steps[n][0], inward, steps[n][1])
                if 0 <= n - lag < len(steps):
                    i, part = steps[n - lag]
                    if not (ahead and part == chunks[i]):
                        pass_on(i, outward, part)

    def arrived(i):
        for way in range(2):

            @pl.when(jnp.logical_not(sends(way)))
            def _():
                for part in range(chunks[i]):
                    take_hop(i, way, part)

            take_hop(i, way, chunks[i])

    for i in range(3):
        loaded(i)
        if i == 0:
            pl.semaphore_wait(barrier, partners)
        end_sends(i, range(chunks[i] + 1))
    last_out(0)
    last_out(1)
    middle(0, 7)
    last_out(2)
    middle(7, 11)
    b[...] = jnp.zeros_like(b)
    u[...] = jnp.zeros_like(u)

    own_slot = [jnp.int32(0)] * PER
    is_own = [jnp.int32(0)] * PER
    got_slot = [jnp.int32(0)] * PER
    got_way = [jnp.int32(0)] * PER
    for q in range(PER):
        for s in range(PER):
            owner, inner = owner_inner(my_y, s)
            here = (owner == my_y) & (inner == q)
            own_slot[q] = jnp.where(here, s, own_slot[q])
            is_own[q] = jnp.where(here, 1, is_own[q])
        for way in range(2):
            for t in range(1, n_y):
                for j in range(t):
                    pair = (j, t) if way == 0 else (n_y - 1 - j, n_y - 1 - t)
                    here = (goes[pair] == 1) & (its_inner[pair] == q) & (my_y == pair[1])
                    slot = jnp.minimum(rank[way, t - 1, j, t], n_slot - 1)
                    got_slot[q] = jnp.where(here, slot, got_slot[q])
                    got_way[q] = jnp.where(here, way, got_way[q])

    group = lane // E
    own_mask = [jnp.full((E, L), is_own[q], jnp.int32) == 1 for q in range(PER)]

    def assembled(i, put, carry=0):
        own, _, rv = fields[i]

        def columns(t, carry):
            at = pl.ds(pl.multiple_of(t * L, L), L)
            parts = []
            for q in range(PER):
                got = rv[got_way[q], got_slot[q], :, at]
                if i == 1:
                    got = jnp.concatenate([got, pltpu.roll(got, E // 2 - 1, 0)], axis=0)
                parts.append(jnp.where(own_mask[q], own[own_slot[q], :, at], got))
            for j in range(PER):
                plane = parts[j]
                for q in range(PER):
                    if q != j:
                        plane = jnp.where(
                            group == q, pltpu.roll(parts[q], (q - j) * E % L, 1), plane
                        )
                carry = put(t * PER + j, j, plane, carry)
            return carry

        return lax.fori_loop(0, E * E // L, columns, carry)

    def at_plane(y):
        return pl.ds(pl.multiple_of(y * E, E), E)

    def base(y):
        return pl.multiple_of(y * ST + ST + 8, 8)

    def padded(y):
        return pl.ds(base(y), E)

    even = (row + lane) % 2 == 0
    odd = (row + lane) % 2 == 1
    pair = lane // 2
    zero = jnp.zeros((E, L), jnp.float32)
    first = ST + 8

    def pack_z(y, v, face):
        return jnp.where(pair == y, pltpu.roll(v, 2 * y + 1, 1), face)

    def pack_all_z(ref):
        def planes(t, face):
            for j in range(4):
                y = t * 4 + j
                face = pack_z(y, ref[padded(y), :], face)
            return face

        return lax.fori_loop(0, E // 4, planes, zero)

    def z_halo(e):
        return jnp.where(lane % 2 == 0, hr[e, 4], pltpu.roll(hr[e, 5], L - 2, 1))

    def z_edge(halo, y):
        return pltpu.roll(halo, lax.rem(L - 2 * y, L), 1)

    def face_copy(e, side):
        axis, step = SIDES[side]
        return pltpu.make_async_remote_copy(
            src_ref=hs.at[e, side],
            dst_ref=hr.at[e, side ^ 1],
            send_sem=hs_sem.at[e, side],
            recv_sem=hr_sem.at[e, side ^ 1],
            device_id={axis: me[axis] + step},
            device_id_type=MESH,
        )

    def send_faces(e, ref, z_face):
        hs[e, 0] = ref[pl.ds(first, E, stride=ST), :]
        hs[e, 1] = ref[pl.ds(first + E - 1, E, stride=ST), :]
        hs[e, 2] = ref[pl.ds(first, E), :]
        hs[e, 3] = ref[pl.ds(first + (E - 1) * ST, E), :]
        hs[e, 4] = z_face
        hs[e, 5] = z_face
        for side in range(6):

            @pl.when(exists(side))
            def _():
                face_copy(e, side).start()

    def wait_faces(e):
        for side in range(6):
            axis, step = SIDES[side]

            @pl.when(exists(side))
            def _():
                pltpu.make_async_remote_copy(
                    src_ref=hs.at[e, side],
                    dst_ref=hr.at[e, side],
                    send_sem=hs_sem.at[e, side],
                    recv_sem=hr_sem.at[e, side],
                    device_id={axis: me[axis] + step},
                    device_id_type=MESH,
                ).wait_recv()

    arrived(0)

    def put_b(y, j, plane, carry):
        b[padded(y), :] = plane
        return carry

    assembled(0, put_b)
    send_faces(0, b, pack_all_z(b))

    loaded(3)
    end_sends(3, (0, 1))
    middle(11, 12)

    arrived(1)

    def put_u(y, j, plane, carry):
        u[padded(y), :] = plane
        return carry

    assembled(1, put_u)
    send_faces(1, u, pack_all_z(u))

    end_sends(3, (2, 3, 4))
    last_out(3)
    middle(12, 14)

    wait_faces(0)
    b[pl.ds(first - 1, E, stride=ST), :] = hr[0, 0]
    b[pl.ds(first + E, E, stride=ST), :] = hr[0, 1]
    b[pl.ds(8, E), :] = hr[0, 2]
    b[pl.ds(first + E * ST, E), :] = hr[0, 3]
    b_halo = z_halo(0)

    def coefs(y, carry):
        v = b[padded(y), :]
        at = at_plane(y)
        edge = z_edge(b_halo, y)
        x_low = 0.5 * (b[pl.ds(base(y) - 1, E), :] + v)
        x_high = 0.5 * (b[pl.ds(base(y) + 1, E), :] + v)
        y_low = 0.5 * (b[padded(y - 1), :] + v)
        y_high = 0.5 * (b[padded(y + 1), :] + v)
        z_low = 0.5 * (jnp.where(lane == 0, edge, pltpu.roll(v, 1, 1)) + v)
        z_high = 0.5 * (jnp.where(lane == L - 1, edge, pltpu.roll(v, L - 1, 1)) + v)
        cxl[at, :] = x_low
        cxh[at, :] = x_high
        cy[at, :] = y_low
        cy[at_plane(y + 1), :] = y_high
        czl[at, :] = jnp.where(lane == 0, 0.0, z_low)
        czh[at, :] = jnp.where(lane == L - 1, 0.0, z_high)
        ez[at, :] = jnp.where(lane == 0, z_low, jnp.where(lane == L - 1, z_high, 0.0))
        dia[at, :] = (x_high + x_low) + (y_high + y_low) + (z_high + z_low)
        return carry

    lax.fori_loop(0, E, coefs, 0)

    middle(14, 16)
    arrived(2)

    def put_a(y, j, plane, carry):
        at = at_plane(y)
        total = plane + dia[at, :]
        inverse = 1.0 / total
        dia[at, :] = total
        inv[at, :] = inverse
        ezi[at, :] = ez[at, :] * inverse
        return carry

    assembled(2, put_a)

    def neighbours(y):
        at = at_plane(y)
        v = u[padded(y), :]
        x_sum = cxh[at, :] * u[pl.ds(base(y) + 1, E), :] + cxl[at, :] * u[pl.ds(base(y) - 1, E), :]
        y_sum = cy[at_plane(y + 1), :] * u[padded(y + 1), :] + cy[at, :] * u[padded(y - 1), :]
        z_sum = czh[at, :] * pltpu.roll(v, L - 1, 1) + czl[at, :] * pltpu.roll(v, 1, 1)
        return v, x_sum + y_sum + z_sum

    low_x = pl.ds(0, E, stride=E)
    high_x = pl.ds(E - 1, E, stride=E)
    low_y = pl.ds(0, E)
    high_y = pl.ds((E - 1) * E, E)
    top_y = pl.ds(E * E, E)

    def add_faces(e):
        for at, term in (
            (low_x, cxl[low_x, :] * hr[e, 0]),
            (high_x, cxh[high_x, :] * hr[e, 1]),
            (low_y, cy[low_y, :] * hr[e, 2]),
            (high_y, cy[top_y, :] * hr[e, 3]),
        ):
            res[at, :] = res[at, :] + term

    middle(16, len(steps) + lag)
    wait_faces(1)
    first_halo = z_halo(1)

    def first_sums(t, carry):
        for j in range(4):
            y = t * 4 + j
            at = at_plane(y)
            res[at, :] = neighbours(y)[1] + ez[at, :] * z_edge(first_halo, y)
        return carry

    lax.fori_loop(0, E // 4, first_sums, 0)
    add_faces(1)
    arrived(3)

    def put_f(y, j, plane, face):
        at = at_plane(y)
        f[at, :] = plane
        new = (plane + res[at, :]) * inv[at, :]
        v = jnp.where(even if j % 2 == 0 else odd, new, u[padded(y), :])
        u[padded(y), :] = v
        return pack_z(y, v, face)

    send_faces(2, u, assembled(3, put_f, zero))

    e = 2
    for sweep in range(SWEEPS):
        for colour in (0, 1):
            if sweep == 0 and colour == 0:
                continue
            masks = (even, odd) if colour == 0 else (odd, even)

            def planes(t, carry):
                for j in range(4):
                    y = t * 4 + j
                    at = at_plane(y)
                    v, total = neighbours(y)
                    new = (f[at, :] + total) * inv[at, :]
                    u[padded(y), :] = jnp.where(masks[j % 2], new, v)
                return carry

            lax.fori_loop(0, E // 4, planes, 0)
            wait_faces(e)
            for at, mask, term in (
                (pl.ds(first, E, stride=ST), 0, cxl[low_x, :] * inv[low_x, :] * hr[e, 0]),
                (pl.ds(first + E - 1, E, stride=ST), 1, cxh[high_x, :] * inv[high_x, :] * hr[e, 1]),
                (pl.ds(first, E), 0, cy[low_y, :] * inv[low_y, :] * hr[e, 2]),
                (pl.ds(first + (E - 1) * ST, E), 1, cy[top_y, :] * inv[high_y, :] * hr[e, 3]),
            ):
                u[at, :] = u[at, :] + jnp.where(masks[mask], term, 0.0)
            halo = z_halo(e)

            def edges(t, face):
                for j in range(4):
                    y = t * 4 + j
                    term = ezi[at_plane(y), :] * z_edge(halo, y)
                    v = u[padded(y), :] + jnp.where(masks[j % 2], term, 0.0)
                    u[padded(y), :] = v
                    face = pack_z(y, v, face)
                return face

            face = lax.fori_loop(0, E // 4, edges, zero)
            e += 1
            send_faces(e, u, face)

    def residual(t, carry):
        for j in range(4):
            y = t * 4 + j
            at = at_plane(y)
            v, total = neighbours(y)
            res[at, :] = f[at, :] - (dia[at, :] * v - total)
        return carry

    lax.fori_loop(0, E // 4, residual, 0)
    for x in range(E):
        sol_out[x] = u[pl.ds(first + x, E, stride=ST), :]
    stores = [pltpu.make_async_copy(sol_out, sol_hbm, out_sem.at[4])]
    stores[0].start()
    wait_faces(e)
    add_faces(e)
    last_halo = z_halo(e)

    def last_edges(t, carry):
        for j in range(4):
            y = t * 4 + j
            at = at_plane(y)
            res[at, :] = res[at, :] + ez[at, :] * z_edge(last_halo, y)
        return carry

    lax.fori_loop(0, E // 4, last_edges, 0)
    for x in range(E):
        res_out[x] = res[pl.ds(x, E, stride=E), :]
        if x % 8 == 7:
            piece = pl.ds(x - 7, 8)
            stores.append(
                pltpu.make_async_copy(res_out.at[piece], res_hbm.at[piece], out_sem.at[x // 8])
            )
            stores[-1].start()

    for i, part in steps:
        for way in range(2):

            @pl.when(sends(way))
            def _():
                hop(i, way, part, my_y + 1 - 2 * way).wait_send()

    for store in stores:
        store.wait()

    for exchange in range(e + 1):
        for side in range(6):

            @pl.when(exists(side))
            def _():
                face_copy(exchange, side).wait_send()


def per_device(width, solution_old, right_side, acoef, bcoef, corners):
    n_y = width["gy"]
    exchanges = 2 + 2 * SWEEPS
    box = (E, E * E)
    field = pltpu.VMEM((E * E, L), jnp.float32)
    padded = pltpu.VMEM(((E + 2) * ST + 16, L), jnp.float32)
    faces = pltpu.VMEM((exchanges, 6, E, L), jnp.float32)
    own = pltpu.VMEM((PER,) + box, jnp.float32)
    moved = pltpu.VMEM((2, n_y - 1) + box, jnp.float32)
    half = pltpu.VMEM((2, n_y - 1, E // 2, E * E), jnp.float32)
    out = jax.ShapeDtypeStruct((E, E, L), jnp.float32)
    return pl.pallas_call(
        functools.partial(kernel, width),
        out_shape=(out, out),
        in_specs=[pl.BlockSpec(memory_space=pltpu.SMEM)]
        + [pl.BlockSpec(memory_space=pl.ANY)] * 4,
        out_specs=(pl.BlockSpec(memory_space=pl.ANY),) * 2,
        scratch_shapes=[own] * 4
        + [moved, half, moved, moved] * 2
        + [padded, padded]
        + [field] * 6
        + [pltpu.VMEM(((E + 1) * E, L), jnp.float32)]
        + [field] * 4
        + [faces] * 2
        + [pltpu.VMEM((E, E, L), jnp.float32)] * 2
        + [pltpu.SemaphoreType.DMA((5,))]
        + [
            pltpu.SemaphoreType.DMA((4, PER)),
            pltpu.SemaphoreType.DMA((4, 2, 5)),
            pltpu.SemaphoreType.DMA((4, 2, 5)),
            pltpu.SemaphoreType.DMA((exchanges, 6)),
            pltpu.SemaphoreType.DMA((exchanges, 6)),
        ],
        compiler_params=pltpu.CompilerParams(
            collective_id=0, has_side_effects=True, vmem_limit_bytes=64 * 1024 * 1024
        ),
        cost_estimate=pl.CostEstimate(
            flops=100 * E * E * L, bytes_accessed=24 * E * E * L, transcendentals=0
        ),
    )(corners, solution_old, right_side, acoef, bcoef)


def solution(mesh):
    width = dict(mesh.shape)
    boxes = P(("gx", "gy", "gz"), None, None)
    level = P("gx", "gy", "gz")
    return jax.shard_map(
        functools.partial(per_device, width),
        mesh=mesh,
        in_specs=(boxes, boxes, boxes, boxes, P()),
        out_specs=(level, level),
        check_vma=False,
    )
```
